512 devices in a mesh: batch: 32 (over z, x), blk: 16 (over y, core).
Axes of the slice: x: 4, y: 8, z: 8, core: 2. Of those that a mesh axis runs over, the one named last changes fastest.
Arguments:
- points: float32 [1024, 16, 3, 256], P('batch', 'blk'), may hold values from -6 to 6
- centers: float32 [1024, 16, 3, 384], P('batch', 'blk'), may hold values from -6 to 6
- exponents: float32 [1024, 16, 384], P('batch', 'blk'), may hold values from 0.1 to 1
- angular: float32 [1024, 16, 3, 384], P('batch', 'blk'), may hold values from -3 to 3
- grid_weights: float32 [1024, 16, 256], P('batch', 'blk'), may hold values from 0.001 to 0.01
- hartree: float32 [1024, 16, 256], P('batch', 'blk'), may hold values from 0 to 1.7
- load_plan: int32 [16, 1024], P('blk'), may hold values from 0 to 1023, each once within a row
- density_blocks: bfloat16 [256, 128, 128], P('blk'), may hold values from -0.046875 to 0.046875
- pair_lists: int32 [32, 16, 16, 2], P('batch', 'blk'), may hold values from 0 to 15
- batch_pairs: int32 [1024, 16, 9], P('batch', 'blk'), may hold values from 0 to 31, as said below
Outputs:
- hamiltonian: float32 [256, 128, 128], P('blk')
- density: float32 [1024, 16, 256], P('batch', 'blk')
The draws below stay inside these ranges and needn't reach their ends.
Inputs may be any that keep to these rules, and one draw needn't show every extreme that they name: Each row of load_plan names every storage row of its column once. `pair_lists`: local index of a block pair within the 16 pairs held by one index of blk. `batch_pairs`: entry e of a device's table is the (e % 2)-th block it reads from index e // 2 of blk; every entry of a device's table is named by some pair of its batches.
All inputs are finite; a program needn't handle non-finite values.
Results may differ from the reference program's by a relative error of at most 0.0065.
Values may be sent and summed in bfloat16 or wider, within the bound.
No kernel may reach another device: no remote copies, remote signals or barrier semaphores. Data moves between devices by JAX's collectives and lax.ppermute only.
A program may use at most 64 MiB of HBM per device.

```python
import math
import jax
import jax.numpy as jnp
from jax import lax

PTS = 256
BSZ = 128
LIST = 3
NBAS = 384
BAT_DEV = 32
CAP = 2
PAIRS_DEV = 16
BATCHES = 1024
COLUMNS = 16
BATCH_RANKS = 32
PAIRS = 256


def draw_batch_pairs(key, part):
    entries = COLUMNS * CAP
    references = BAT_DEV * LIST * LIST

    def one_device(device_key):
        first_key, second_key = jax.random.split(device_key)
        extra = jax.random.randint(first_key, (references - entries,), 0, entries, dtype=jnp.int32)
        listed = jnp.concatenate([jnp.arange(entries, dtype=jnp.int32), extra])
        return jax.random.permutation(second_key, listed)
    device_keys = jax.random.split(key, BATCH_RANKS * COLUMNS)
    values = jax.vmap(one_device)(device_keys)
    values = values.reshape(BATCH_RANKS, COLUMNS, BAT_DEV, LIST * LIST)
    return jnp.transpose(values, (0, 2, 1, 3)).reshape(BATCHES, COLUMNS, LIST * LIST)


def with_ends(values, own_key, least, largest):
    place = [jax.random.randint(jax.random.fold_in(own_key, axis), (), 0, length) for axis, length in enumerate(values.shape)]
    main_axis = values.shape.index(max(values.shape))
    next_to = place[:main_axis] + [(place[main_axis] + 1) % values.shape[main_axis]] + place[main_axis + 1:]
    return values.at[tuple(place)].set(least).at[tuple(next_to)].set(largest)


def block_scale(stream_key, dims, pieces, smallest, top_value):
    def one(position, blocks):
        steps = jax.random.uniform(jax.random.fold_in(jax.random.fold_in(stream_key, 6), position), (blocks,), jnp.float32, smallest / len(pieces), top_value / len(pieces))
        return jnp.repeat(jnp.exp(steps), dims[position] // blocks).reshape((-1,) + (1,) * (len(dims) - position - 1))

    loudness = one(*pieces[0])
    for cut in pieces[1:]:
        loudness = loudness * one(*cut)
    return loudness


def scatter_about(rng, shape, spread, limit, pieces=(), kind=jnp.bfloat16):
    values = jax.random.normal(rng, shape, jnp.float32) * spread
    if len(pieces) > 0:
        values = block_scale(rng, shape, pieces, -0.22, 0.18) * values
    return jnp.clip(values, min=-limit, max=limit).astype(kind)


def setup_inputs(seed: int = 0) -> dict:
    streams_of = jax.random.split(jax.random.key(seed), 11)
    return {
        "points": scatter_about(streams_of[0], (BATCHES, COLUMNS, 3, PTS), 1.0, 6.0, ((0, 32), (1, 16)), jnp.float32),
        "centers": scatter_about(streams_of[1], (BATCHES, COLUMNS, 3, NBAS), 1.0, 6.0, ((0, 32), (1, 16)), jnp.float32),
        "exponents": jnp.clip(jnp.exp(math.log(1.0) - 2.3025851 * jax.random.uniform(streams_of[2], (BATCHES, COLUMNS, NBAS), jnp.float32) ** block_scale(streams_of[2], (BATCHES, COLUMNS, NBAS), ((0, 32), (1, 16)), -0.2, 0.2)), 0.1, 1.0),
        "angular": scatter_about(streams_of[3], (BATCHES, COLUMNS, 3, NBAS), 0.5, 3.0, ((0, 32), (1, 16)), jnp.float32),
        "grid_weights": jnp.clip(jnp.exp(math.log(0.01) - 2.30258502 * jax.random.uniform(streams_of[4], (BATCHES, COLUMNS, PTS), jnp.float32) ** block_scale(streams_of[4], (BATCHES, COLUMNS, PTS), ((0, 32), (1, 16)), -0.2, 0.2)), 0.001, 0.01),
        "hartree": jnp.clip(1.7 * jax.random.uniform(streams_of[5], (BATCHES, COLUMNS, PTS), jnp.float32) ** block_scale(streams_of[5], (BATCHES, COLUMNS, PTS), ((0, 32), (1, 16)), -0.2, 0.2), 0.0, 1.7),
        "load_plan": jax.vmap(lambda own: jax.random.permutation(own, BATCHES))(jax.random.split(streams_of[6], COLUMNS)).reshape((COLUMNS, BATCHES)).astype(jnp.int32),
        "density_blocks": scatter_about(streams_of[7], (PAIRS, BSZ, BSZ), (NBAS * 48) ** -0.5, 0.046875, ((0, 16),)),
        "pair_lists": with_ends(jax.random.randint(streams_of[8], (BATCH_RANKS, COLUMNS, COLUMNS, CAP), 0, PAIRS_DEV), jax.random.fold_in(streams_of[8], 1), 0, PAIRS_DEV - 1).astype(jnp.int32),
        "batch_pairs": draw_batch_pairs(jax.random.fold_in(streams_of[10], 71), 0),
    }


xc_scale = 0.98474502
soft_square = 0.01


def exchange_potential(grid_rho):
    return -xc_scale * jnp.power(grid_rho * grid_rho + soft_square, 1.0 / 6.0)


def evaluate(points, centers, exponents, angular):
    distance = jnp.zeros(points.shape[:-2] + (points.shape[-1], centers.shape[-1]), jnp.float32)
    angular_part = jnp.ones_like(distance)
    for component in range(3):
        delta = points[..., component, :, None] - centers[..., component, None, :]
        distance = distance + delta * delta
        angular_part = angular_part + angular[..., component, None, :] * delta
    return (jnp.exp(-exponents[..., None, :] * distance) * angular_part).astype(jnp.bfloat16)


def reference(points, centers, exponents, angular, grid_weights, hartree, load_plan, density_blocks, pair_lists, batch_pairs):
    col_ids = jnp.arange(COLUMNS, dtype=jnp.int32)
    source = jnp.transpose(load_plan).astype(jnp.int32)
    potential = hartree[source, col_ids[None, :]]
    owners = jnp.arange(COLUMNS * CAP, dtype=jnp.int32) // CAP
    tables = owners[None, None, :] * PAIRS_DEV + pair_lists.astype(jnp.int32).reshape(BATCH_RANKS, COLUMNS, COLUMNS * CAP)
    rank_of_row = jnp.arange(BATCHES, dtype=jnp.int32) // BAT_DEV
    pair_ids = tables[rank_of_row[:, None, None], col_ids[None, :, None], batch_pairs.astype(jnp.int32)]
    slot_total = BATCHES * COLUMNS

    def flatten(value):
        return value.reshape((slot_total,) + value.shape[2:])

    def integrate(running, item):
        point_row, center_row, decay_rates, slope_terms, weight_row, pot_row, pair_row = item
        basis = evaluate(point_row, center_row, decay_rates, slope_terms)
        blocks = density_blocks[pair_row]
        sub_density = blocks.reshape(LIST, LIST, BSZ, BSZ).transpose(0, 2, 1, 3).reshape(NBAS, NBAS)
        inner = jnp.dot(basis, sub_density, preferred_element_type=jnp.float32)
        grid_rho = jnp.sum(inner * basis.astype(jnp.float32), axis=-1)
        effective = pot_row + exchange_potential(grid_rho)
        scaled = ((weight_row * effective)[:, None] * basis.astype(jnp.float32)).astype(jnp.bfloat16)
        full_blocks = jnp.dot(jnp.transpose(basis), scaled, preferred_element_type=jnp.float32)
        contributions = full_blocks.reshape(LIST, BSZ, LIST, BSZ).transpose(0, 2, 1, 3).reshape(LIST * LIST, BSZ, BSZ)
        return running.at[pair_row].add(contributions), grid_rho

    zero_table = jnp.zeros((PAIRS, BSZ, BSZ), jnp.float32)
    items = (flatten(points), flatten(centers), flatten(exponents), flatten(angular), flatten(grid_weights), flatten(potential), flatten(pair_ids))
    hamiltonian, rho_rows = lax.scan(integrate, zero_table, items)
    grid_rho = rho_rows.reshape(BATCHES, COLUMNS, PTS)
    density = jnp.zeros((BATCHES, COLUMNS, PTS), jnp.float32).at[source, col_ids[None, :]].set(grid_rho)
    return (hamiltonian, density)
```

```python
import jax
import jax.numpy as jnp
from jax import lax
from jax.experimental import pallas as pl
from jax.experimental.pallas import tpu as pltpu
from jax.sharding import PartitionSpec as P

LIST = 3
xc_scale = 0.98474502
soft_square = 0.01
log2_e = 1.4426950408889634

bf16 = jnp.bfloat16
f32 = jnp.float32
VMEM = pl.BlockSpec(memory_space=pltpu.VMEM)
SMEM = pl.BlockSpec(memory_space=pltpu.SMEM)


def call(body, outs, ins, scratch=(), flops=0, moved=0, limit=24):
    return pl.pallas_call(
        body,
        out_shape=outs,
        in_specs=ins,
        out_specs=jax.tree.map(lambda _: VMEM, outs),
        scratch_shapes=list(scratch),
        compiler_params=pltpu.CompilerParams(vmem_limit_bytes=limit * 2**20),
        cost_estimate=pl.CostEstimate(flops=flops, bytes_accessed=moved, transcendentals=0),
    )


def basis_kernel(points_ref, params_ref, out_ref):
    slots, width, _ = out_ref.shape
    step = 32

    def one(s, carry):
        columns = jnp.transpose(params_ref[s])
        for at in range(0, width, step):
            own = columns[at : at + step]
            distance = None
            angular = None
            for a in range(3):
                delta = points_ref[s, a : a + 1, :] - own[:, a : a + 1]
                square = delta * delta
                slope = own[:, 4 + a : 5 + a] * delta
                distance = square if a == 0 else distance + square
                angular = slope + 1.0 if a == 0 else angular + slope
            value = jnp.exp2((own[:, 3:4] * -log2_e) * distance) * angular
            out_ref[s, at : at + step, :] = value.astype(bf16)
        return carry

    lax.fori_loop(0, slots, one, 0)


def pick_kernel(asked_ref, blocks_ref, out_ref):
    for e in range(out_ref.shape[0]):
        out_ref[e] = blocks_ref[asked_ref[e]]


def integrate_kernel(
    pairs_ref, plan_ref, basis_ref, table_ref, hartree_ref, weights_ref,
    out_ref, rho_ref, sub_ref, sums_ref,
):
    slots = basis_ref.shape[0]
    entries, block, _ = table_ref.shape
    unroll = sub_ref.shape[0]

    def clear(e, carry):
        sums_ref[e] = jnp.zeros((block, block), f32)
        return carry

    lax.fori_loop(0, entries, clear, 0)

    def group(turn, carry):
        for u in range(unroll):
            s = turn * unroll + u
            for k in range(LIST):
                for l in range(LIST):
                    sub_ref[u, k * block : (k + 1) * block, l * block : (l + 1) * block] = table_ref[
                        pairs_ref[s * LIST * LIST + k * LIST + l]
                    ]
        for u in range(unroll):
            s = turn * unroll + u
            basis = basis_ref[s]
            inner = jnp.dot(sub_ref[u], basis, preferred_element_type=f32)
            wide = basis.astype(f32)
            rho = jnp.sum(inner * wide, axis=0, keepdims=True)
            rho_ref[pl.ds(s, 1), :] = rho
            root = jnp.exp2(jnp.log2(rho * rho + soft_square) * (1.0 / 6.0))
            effective = hartree_ref[pl.ds(plan_ref[s], 1), :] - xc_scale * root
            scaled = (wide * (weights_ref[pl.ds(s, 1), :] * effective)).astype(bf16)
            full = lax.dot_general(
                basis, scaled, (((1,), (1,)), ((), ())), preferred_element_type=f32
            )
            for k in range(LIST):
                for l in range(LIST):
                    e = pairs_ref[s * LIST * LIST + k * LIST + l]
                    sums_ref[e] += full[
                        k * block : (k + 1) * block, l * block : (l + 1) * block
                    ]
        return carry

    lax.fori_loop(0, slots // unroll, group, 0)

    low = lax.broadcasted_iota(jnp.int32, (1, 8, block), 1) < 4
    for c in range(out_ref.shape[2]):
        first = sums_ref[2 * c].reshape(block // 8, 8, block)
        second = sums_ref[2 * c + 1].reshape(block // 8, 8, block)
        out_ref[:, 0, c] = jnp.where(low, first, pltpu.roll(second, 4, 1)).astype(bf16)
        out_ref[:, 1, c] = jnp.where(low, pltpu.roll(first, 4, 1), second).astype(bf16)


def add_kernel(target_ref, received_ref, out_ref):
    rows = out_ref.shape[1]
    length = target_ref.shape[1]
    chosen = lax.broadcasted_iota(jnp.int32, (rows, length), 0) == target_ref[...]
    total = jnp.dot(
        chosen.astype(f32).astype(bf16), received_ref[...], preferred_element_type=f32
    ).astype(bf16)
    for h in range(out_ref.shape[0]):
        out_ref[h] = total


def merge_kernel(received_ref, out_ref):
    half, _, rows, block = received_ref.shape
    low = lax.broadcasted_iota(jnp.int32, (1, 8, block), 1) < 4
    for at in range(0, rows, 16):
        even = received_ref[:, 0, at : at + 16, :].astype(f32)
        odd = received_ref[:, 1, at : at + 16, :].astype(f32)
        for q in range(2):
            first = even[:, 8 * q : 8 * q + 8]
            second = odd[:, 8 * q : 8 * q + 8]
            place = at // 4 + 2 * q
            out_ref[place] = jnp.where(low, first, pltpu.roll(second, 4, 1)).reshape(8 * half, block)
            out_ref[place + 1] = jnp.where(low, pltpu.roll(first, 4, 1), second).reshape(
                8 * half, block
            )


def to_all(value, axis):
    copies = jnp.broadcast_to(value[None], (lax.axis_size(axis),) + value.shape)
    return lax.all_to_all(copies, axis, split_axis=0, concat_axis=0, tiled=True)


def on_device(
    points,
    centers,
    exponents,
    angular,
    grid_weights,
    hartree,
    load_plan,
    density_blocks,
    pair_lists,
    batch_pairs,
):
    slots, _, _, grid = points.shape
    ranks = lax.axis_size("batch")
    columns = lax.axis_size("blk")
    per_owner = pair_lists.shape[3]
    held, block, _ = density_blocks.shape
    entries = columns * per_owner
    width = LIST * block
    piece = block // ranks
    rank = lax.axis_index("batch")
    plan_rows = lax.dynamic_slice_in_dim(load_plan[0], rank * slots, slots)

    wanted = pair_lists[0, 0]
    asked = lax.all_to_all(wanted, "blk", split_axis=0, concat_axis=0, tiled=True)
    stored = to_all(hartree[:, 0, :], "batch").reshape(ranks * slots, grid)

    params = jnp.concatenate(
        [centers[:, 0], exponents, angular[:, 0], jnp.zeros((slots, 1, width), f32)], axis=1
    )
    basis = call(
        basis_kernel,
        jax.ShapeDtypeStruct((slots, width, grid), bf16),
        [VMEM, VMEM],
        flops=slots * width * grid * 400,
        moved=slots * width * grid * 2,
    )(points[:, 0], params)

    sent = call(
        pick_kernel,
        jax.ShapeDtypeStruct((entries, block, block), bf16),
        [SMEM, VMEM],
        moved=entries * block * block * 4,
    )(asked.reshape(entries), density_blocks)
    table = lax.all_to_all(
        sent.reshape(columns, per_owner * block, block), "blk", split_axis=0, concat_axis=0, tiled=True
    ).reshape(entries, block, block)

    everyone = to_all(asked, "batch").reshape(ranks * entries, 1)
    targets = (everyone * piece + jnp.arange(piece, dtype=jnp.int32)[None]).reshape(
        1, ranks * entries * piece
    )

    unroll = 2
    partial, rho = call(
        integrate_kernel,
        (
            jax.ShapeDtypeStruct((ranks // 2, 2, columns, per_owner * piece, block), bf16),
            jax.ShapeDtypeStruct((slots, grid), f32),
        ),
        [SMEM, SMEM, VMEM, VMEM, VMEM, VMEM],
        [pltpu.VMEM((unroll, width, width), bf16), pltpu.VMEM((entries, block, block), f32)],
        flops=slots * width * width * grid * 4,
        moved=slots * width * grid * 2,
    )(
        batch_pairs.reshape(slots * LIST * LIST), plan_rows, basis, table, stored, grid_weights[:, 0]
    )

    rows = per_owner * piece
    received = lax.all_to_all(
        partial.reshape(ranks * columns, rows, block),
        ("batch", "blk"),
        split_axis=0,
        concat_axis=0,
        tiled=True,
    ).reshape(ranks * columns * rows, block)
    spread = to_all(rho.astype(bf16), "batch").reshape(ranks * slots, grid)

    totals = call(
        add_kernel,
        jax.ShapeDtypeStruct((ranks, held * piece, block), bf16),
        [VMEM, VMEM],
        moved=ranks * columns * rows * block * 2,
    )(targets, received)
    gathered = lax.all_to_all(totals, "batch", split_axis=0, concat_axis=0, tiled=True)
    hamiltonian = call(
        merge_kernel,
        jax.ShapeDtypeStruct((held, block, block), f32),
        [VMEM],
        moved=held * block * block * 6,
    )(gathered.reshape(ranks // 2, 2, held * piece, block))

    own_rows = rank * slots + jnp.arange(slots, dtype=jnp.int32)
    placement = (own_rows[:, None] == load_plan).astype(bf16)
    density = jnp.dot(placement, spread, preferred_element_type=f32)
    return (hamiltonian, density[:, None, :])


def solution(mesh):
    return jax.shard_map(
        on_device,
        mesh=mesh,
        in_specs=(
            P("batch", "blk", None, None),
            P("batch", "blk", None, None),
            P("batch", "blk", None),
            P("batch", "blk", None, None),
            P("batch", "blk", None),
            P("batch", "blk", None),
            P("blk", None),
            P("blk", None, None),
            P("batch", "blk", None, None),
            P("batch", "blk", None),
        ),
        out_specs=(P("blk", None, None), P("batch", "blk", None)),
        check_vma=False,
    )
```

```python
import jax
import jax.numpy as jnp
from jax import lax
from jax.experimental import pallas as pl
from jax.experimental.pallas import tpu as pltpu
from jax.sharding import PartitionSpec as P

LIST = 3
BLK = ("y", "core")
xc_scale = 0.98474502
soft_square = 0.01
log2_e = 1.4426950408889634

bf16 = jnp.bfloat16
f32 = jnp.float32
VMEM = pl.BlockSpec(memory_space=pltpu.VMEM)
HBM = pl.BlockSpec(memory_space=pltpu.HBM)
SMEM = pl.BlockSpec(memory_space=pltpu.SMEM)


def rows_of(*block):
    return pl.BlockSpec(block, lambda n: (n,) + (0,) * (len(block) - 1))


def call(body, outs, ins, scratch=(), flops=0, moved=0, limit=24, grid=(), out_specs=None):
    return pl.pallas_call(
        body,
        out_shape=outs,
        grid=grid,
        in_specs=ins,
        out_specs=out_specs or jax.tree.map(lambda _: VMEM, outs),
        scratch_shapes=list(scratch),
        compiler_params=pltpu.CompilerParams(vmem_limit_bytes=limit * 2**20),
        cost_estimate=pl.CostEstimate(flops=flops, bytes_accessed=moved, transcendentals=0),
    )


def basis_kernel(points_ref, params_ref, out_ref, done_ref):
    slots, width, _ = out_ref.shape
    step = 32
    done_ref[...] = jnp.zeros_like(done_ref)

    def one(s, carry):
        columns = jnp.transpose(params_ref[s])
        for at in range(0, width, step):
            own = columns[at : at + step]
            distance = None
            angular = None
            for a in range(3):
                delta = points_ref[s, a : a + 1, :] - own[:, a : a + 1]
                square = delta * delta
                slope = own[:, 4 + a : 5 + a] * delta
                distance = square if a == 0 else distance + square
                angular = slope + 1.0 if a == 0 else angular + slope
            value = jnp.exp2((own[:, 3:4] * -log2_e) * distance) * angular
            out_ref[s, at : at + step, :] = value.astype(bf16)
        return carry

    lax.fori_loop(0, slots, one, 0)


def pick_kernel(places_ref, blocks_ref, done_ref, own_ref, other_ref, sems):
    del done_ref
    half = own_ref.shape[0]
    copies = []
    for n in range(2 * half):
        to = other_ref.at[n] if n < half else own_ref.at[n - half]
        copies.append(pltpu.make_async_copy(blocks_ref.at[places_ref[n]], to, sems.at[n]))
    for copy in copies:
        copy.start()
    for copy in copies:
        copy.wait()


def density_kernel(pairs_ref, core_ref, basis_ref, own_ref, other_ref, rho_ref, table_ref, sub_ref):
    slots = basis_ref.shape[0]
    half, block, _ = own_ref.shape
    unroll = sub_ref.shape[0]
    start = pl.program_id(0) * slots

    @pl.when(start == 0)
    def _():
        core = core_ref[0]
        for n in range(half):
            base = 4 * (n // 2) + n % 2
            table_ref[base + 2 * core] = own_ref[n]
            table_ref[base + 2 * (1 - core)] = other_ref[n]

    def group(turn, carry):
        for u in range(unroll):
            s = turn * unroll + u
            for k in range(LIST):
                for l in range(LIST):
                    sub_ref[u, k * block : (k + 1) * block, l * block : (l + 1) * block] = table_ref[
                        pairs_ref[(start + s) * LIST * LIST + k * LIST + l]
                    ]
        for u in range(unroll):
            s = turn * unroll + u
            basis = basis_ref[s]
            inner = jnp.dot(sub_ref[u], basis, preferred_element_type=f32)
            rho_ref[pl.ds(start + s, 1), :] = jnp.sum(inner * basis.astype(f32), axis=0, keepdims=True)
        return carry

    lax.fori_loop(0, slots // unroll, group, 0)


def matrix_kernel(
    pairs_ref, plan_ref, basis_ref, rho_ref, hartree_ref, weights_ref,
    out_ref, lists_ref, sums_ref, factor_ref,
):
    slots = basis_ref.shape[0]
    total = rho_ref.shape[0]
    entries, block, _ = sums_ref.shape
    stride = hartree_ref.shape[0] // lists_ref.shape[0]
    unroll = 2
    start = pl.program_id(0) * slots

    @pl.when(start == 0)
    def _():
        for r in range(lists_ref.shape[0]):
            at = r * stride + total
            lists_ref[r : r + 1, :] = hartree_ref[at : at + 1, :block]
        for s in range(total):
            at = plan_ref[s]
            factor_ref[s : s + 1, :] = hartree_ref[
                pl.ds(lax.div(at, total) * stride + lax.rem(at, total), 1), :
            ]
        rho = rho_ref[...]
        root = jnp.exp2(jnp.log2(rho * rho + soft_square) * (1.0 / 6.0))
        factor_ref[...] = weights_ref[...] * (factor_ref[...] - xc_scale * root)

        def clear(e, carry):
            sums_ref[e] = jnp.zeros((block, block), f32)
            return carry

        lax.fori_loop(0, entries, clear, 0)

    def group(turn, carry):
        for u in range(unroll):
            s = turn * unroll + u
            basis = basis_ref[s]
            scaled = (basis.astype(f32) * factor_ref[pl.ds(start + s, 1), :]).astype(bf16)
            full = lax.dot_general(
                basis, scaled, (((1,), (1,)), ((), ())), preferred_element_type=f32
            )
            for k in range(LIST):
                for l in range(LIST):
                    e = pairs_ref[(start + s) * LIST * LIST + k * LIST + l]
                    sums_ref[e] += full[
                        k * block : (k + 1) * block, l * block : (l + 1) * block
                    ]
        return carry

    lax.fori_loop(0, slots // unroll, group, 0)

    @pl.when(start == total - slots)
    def _():
        low = lax.broadcasted_iota(jnp.int32, (1, 8, block), 1) < 4
        for c in range(out_ref.shape[2]):
            first = sums_ref[2 * c].reshape(block // 8, 8, block)
            second = sums_ref[2 * c + 1].reshape(block // 8, 8, block)
            out_ref[:, 0, c] = jnp.where(low, first, pltpu.roll(second, 4, 1)).astype(bf16)
            out_ref[:, 1, c] = jnp.where(low, pltpu.roll(first, 4, 1), second).astype(bf16)


def add_kernel(target_ref, received_ref, rho_ref, out_ref):
    block = out_ref.shape[2]
    parts = rho_ref.shape[1] // block
    slots = rho_ref.shape[0]
    rows = out_ref.shape[1] - parts * slots
    length = target_ref.shape[1]
    chosen = lax.broadcasted_iota(jnp.int32, (rows, length), 0) == target_ref[...]
    total = jnp.dot(
        chosen.astype(f32).astype(bf16), received_ref[...], preferred_element_type=f32
    ).astype(bf16)
    rho = rho_ref[...].astype(bf16)
    for h in range(out_ref.shape[0]):
        out_ref[h, :rows, :] = total
        for n in range(parts):
            out_ref[h, rows + n * slots : rows + (n + 1) * slots, :] = rho[
                :, n * block : (n + 1) * block
            ]


def merge_kernel(received_ref, plan_ref, rank_ref, out_ref, density_ref):
    half, _, rows, block = received_ref.shape
    slots = density_ref.shape[0]
    parts = density_ref.shape[1] // block
    rows -= parts * slots
    low = lax.broadcasted_iota(jnp.int32, (1, 8, block), 1) < 4
    for at in range(0, rows, 16):
        even = received_ref[:, 0, at : at + 16, :].astype(f32)
        odd = received_ref[:, 1, at : at + 16, :].astype(f32)
        for q in range(2):
            first = even[:, 8 * q : 8 * q + 8]
            second = odd[:, 8 * q : 8 * q + 8]
            place = at // 4 + 2 * q
            out_ref[place] = jnp.where(low, first, pltpu.roll(second, 4, 1)).reshape(8 * half, block)
            out_ref[place + 1] = jnp.where(low, pltpu.roll(first, 4, 1), second).reshape(
                8 * half, block
            )
    length = plan_ref.shape[1]
    own = lax.broadcasted_iota(jnp.int32, (slots, length), 0) + rank_ref[0] * slots
    chosen = (own == plan_ref[...]).astype(f32).astype(bf16)
    for n in range(parts):
        values = received_ref[:, :, rows + n * slots : rows + (n + 1) * slots, :]
        density_ref[:, n * block : (n + 1) * block] = jnp.dot(
            chosen, values.reshape(length, block), preferred_element_type=f32
        )


def to_all(value, axis):
    copies = jnp.broadcast_to(value[None], (lax.axis_size(axis),) + value.shape)
    return lax.all_to_all(copies, axis, split_axis=0, concat_axis=0, tiled=True)


def on_device(
    points,
    centers,
    exponents,
    angular,
    grid_weights,
    hartree,
    load_plan,
    density_blocks,
    pair_lists,
    batch_pairs,
):
    slots, _, _, grid = points.shape
    ranks = lax.axis_size("batch")
    columns = lax.axis_size(BLK)
    per_owner = pair_lists.shape[3]
    held, block, _ = density_blocks.shape
    entries = columns * per_owner
    width = LIST * block
    piece = block // ranks
    rank = lax.axis_index("batch")
    core = lax.axis_index("core")
    swap = [(0, 1), (1, 0)]
    plan_rows = lax.dynamic_slice_in_dim(load_plan[0], rank * slots, slots)

    near = lax.all_gather(density_blocks, "y", axis=0, tiled=True)
    wanted = pair_lists[0, 0]
    asked = lax.ppermute(wanted, "core", swap)

    listed = jnp.pad(wanted.reshape(1, entries).astype(f32), ((0, 7), (0, grid - entries)))
    stored = to_all(jnp.concatenate([hartree[:, 0], listed]), "batch")
    stride = stored.shape[1]
    stored = stored.reshape(ranks * stride, grid)

    params = jnp.concatenate(
        [centers[:, 0], exponents, angular[:, 0], jnp.zeros((slots, 1, width), f32)], axis=1
    )
    group = min(4, slots)
    steps = (slots // group,)
    basis, done = call(
        basis_kernel,
        (jax.ShapeDtypeStruct((slots, width, grid), bf16), jax.ShapeDtypeStruct((8, block), f32)),
        [rows_of(group, 3, grid), rows_of(group, 8, width)],
        grid=steps,
        out_specs=(rows_of(group, width, grid), VMEM),
        limit=48,
        flops=slots * width * grid * 400,
        moved=slots * width * grid * 2,
    )(points[:, 0], params)

    sides = jnp.stack([asked, wanted]).reshape(2, columns // 2, 2, per_owner)
    sides = lax.dynamic_index_in_dim(sides, core, 2, keepdims=False)
    sides = sides + held * jnp.arange(columns // 2, dtype=jnp.int32)[None, :, None]
    half = jax.ShapeDtypeStruct((entries // 2, block, block), bf16)
    own, other = call(
        pick_kernel,
        (half, half),
        [SMEM, HBM, HBM],
        [pltpu.SemaphoreType.DMA((entries,))],
        limit=60,
        moved=entries * block * block * 4,
    )(sides.reshape(entries), near, done)
    other = lax.ppermute(other, "core", swap)

    pairs = batch_pairs.reshape(slots * LIST * LIST)
    unroll = 2
    rho = call(
        density_kernel,
        jax.ShapeDtypeStruct((slots, grid), f32),
        [SMEM, SMEM, rows_of(group, width, grid), VMEM, VMEM],
        [pltpu.VMEM((entries, block, block), bf16), pltpu.VMEM((unroll, width, width), bf16)],
        grid=steps,
        limit=48,
        flops=slots * width * width * grid * 2,
        moved=slots * width * grid * 2,
    )(pairs, core.reshape(1), basis, own, other)
    partial, lists = call(
        matrix_kernel,
        (
            jax.ShapeDtypeStruct((ranks // 2, 2, columns, per_owner * piece, block), bf16),
            jax.ShapeDtypeStruct((ranks, block), f32),
        ),
        [SMEM, SMEM, rows_of(group, width, grid), VMEM, VMEM, VMEM],
        [pltpu.VMEM((entries, block, block), f32), pltpu.VMEM((slots, grid), f32)],
        grid=steps,
        limit=48,
        flops=slots * width * width * grid * 2,
        moved=slots * width * grid * 2,
    )(pairs, plan_rows, basis, rho, stored, grid_weights[:, 0])

    rows = per_owner * piece
    received = lax.all_to_all(
        partial.reshape(ranks * columns, rows, block),
        ("batch",) + BLK,
        split_axis=0,
        concat_axis=0,
        tiled=True,
    ).reshape(ranks * columns * rows, block)

    asking = lax.all_gather(lists, BLK, axis=0)
    asking = lax.dynamic_slice_in_dim(asking, lax.axis_index(BLK) * per_owner, per_owner, 2)
    asking = asking.astype(jnp.int32).transpose(1, 0, 2).reshape(ranks * entries, 1)
    targets = (asking * piece + jnp.arange(piece, dtype=jnp.int32)[None]).reshape(
        1, ranks * entries * piece
    )

    lines = held * piece + slots * grid // block
    totals = call(
        add_kernel,
        jax.ShapeDtypeStruct((ranks, lines, block), bf16),
        [VMEM, VMEM, VMEM],
        moved=ranks * columns * rows * block * 2,
    )(targets, received, rho)
    gathered = lax.all_to_all(totals, "batch", split_axis=0, concat_axis=0, tiled=True)
    hamiltonian, density = call(
        merge_kernel,
        (
            jax.ShapeDtypeStruct((held, block, block), f32),
            jax.ShapeDtypeStruct((slots, grid), f32),
        ),
        [VMEM, VMEM, SMEM],
        moved=held * block * block * 6,
    )(gathered.reshape(ranks // 2, 2, lines, block), load_plan, rank.reshape(1))
    return (hamiltonian, density[:, None, :])


def solution(mesh):
    ranks, columns = mesh.devices.shape
    fine = jax.sharding.Mesh(mesh.devices.reshape(ranks, columns // 2, 2), ("batch",) + BLK)
    return jax.shard_map(
        on_device,
        mesh=fine,
        in_specs=(
            P("batch", BLK, None, None),
            P("batch", BLK, None, None),
            P("batch", BLK, None),
            P("batch", BLK, None, None),
            P("batch", BLK, None),
            P("batch", BLK, None),
            P(BLK, None),
            P(BLK, None, None),
            P("batch", BLK, None, None),
            P("batch", BLK, None),
        ),
        out_specs=(P(BLK, None, None), P("batch", BLK, None)),
        check_vma=False,
    )
```

```python
import jax
import jax.numpy as jnp
from jax import lax
from jax.experimental import pallas as pl
from jax.experimental.pallas import tpu as pltpu
from jax.sharding import PartitionSpec as P

LIST = 3
xc_scale = 0.98474502
soft_square = 0.01
log2_e = 1.4426950408889634

bf16 = jnp.bfloat16
f32 = jnp.float32
VMEM = pl.BlockSpec(memory_space=pltpu.VMEM)
HBM = pl.BlockSpec(memory_space=pltpu.HBM)
SMEM = pl.BlockSpec(memory_space=pltpu.SMEM)


def rows_of(*block):
    return pl.BlockSpec(block, lambda n: (n,) + (0,) * (len(block) - 1))


def call(body, outs, ins, scratch=(), flops=0, moved=0, limit=24, grid=(), out_specs=None):
    return pl.pallas_call(
        body,
        out_shape=outs,
        grid=grid,
        in_specs=ins,
        out_specs=out_specs or jax.tree.map(lambda _: VMEM, outs),
        scratch_shapes=list(scratch),
        compiler_params=pltpu.CompilerParams(vmem_limit_bytes=limit * 2**20),
        cost_estimate=pl.CostEstimate(flops=flops, bytes_accessed=moved, transcendentals=0),
    )


def basis_kernel(points_ref, params_ref, out_ref, done_ref):
    slots, width, _ = out_ref.shape
    step = 32
    done_ref[...] = jnp.zeros_like(done_ref)

    def one(s, carry):
        columns = jnp.transpose(params_ref[s])
        for at in range(0, width, step):
            own = columns[at : at + step]
            distance = None
            angular = None
            for a in range(3):
                delta = points_ref[s, a : a + 1, :] - own[:, a : a + 1]
                square = delta * delta
                slope = own[:, 4 + a : 5 + a] * delta
                distance = square if a == 0 else distance + square
                angular = slope + 1.0 if a == 0 else angular + slope
            value = jnp.exp2((own[:, 3:4] * -log2_e) * distance) * angular
            out_ref[s, at : at + step, :] = value.astype(bf16)
        return carry

    lax.fori_loop(0, slots, one, 0)


def pick_kernel(asked_ref, blocks_ref, out_ref):
    for e in range(out_ref.shape[0]):
        out_ref[e] = blocks_ref[asked_ref[e]]


def spread_kernel(hartree_ref, listed_ref, done_ref, out_ref):
    del done_ref
    slots = hartree_ref.shape[0]
    out_ref[:slots] = hartree_ref[...]
    out_ref[slots:] = jnp.broadcast_to(listed_ref[...], (out_ref.shape[0] - slots, out_ref.shape[1]))


def density_kernel(pairs_ref, basis_ref, table_ref, rho_ref, sub_ref):
    slots = basis_ref.shape[0]
    block = table_ref.shape[1]
    unroll = sub_ref.shape[0]
    start = pl.program_id(0) * slots

    def group(turn, carry):
        for u in range(unroll):
            s = turn * unroll + u
            for k in range(LIST):
                for l in range(LIST):
                    sub_ref[u, k * block : (k + 1) * block, l * block : (l + 1) * block] = table_ref[
                        pairs_ref[(start + s) * LIST * LIST + k * LIST + l]
                    ]
        for u in range(unroll):
            s = turn * unroll + u
            basis = basis_ref[s]
            inner = jnp.dot(sub_ref[u], basis, preferred_element_type=f32)
            rho_ref[pl.ds(start + s, 1), :] = jnp.sum(inner * basis.astype(f32), axis=0, keepdims=True)
        return carry

    lax.fori_loop(0, slots // unroll, group, 0)


def matrix_kernel(
    pairs_ref, plan_ref, basis_ref, rho_ref, hartree_ref, weights_ref,
    out_ref, lists_ref, sums_ref, factor_ref,
):
    slots = basis_ref.shape[0]
    total = rho_ref.shape[0]
    entries, block, _ = sums_ref.shape
    stride = hartree_ref.shape[0] // lists_ref.shape[0]
    unroll = 2
    start = pl.program_id(0) * slots

    @pl.when(start == 0)
    def _():
        for r in range(lists_ref.shape[0]):
            at = r * stride + total
            lists_ref[r : r + 1, :] = hartree_ref[at : at + 1, :block]
        for s in range(total):
            at = plan_ref[s]
            factor_ref[s : s + 1, :] = hartree_ref[
                pl.ds(lax.div(at, total) * stride + lax.rem(at, total), 1), :
            ]
        rho = rho_ref[...]
        root = jnp.exp2(jnp.log2(rho * rho + soft_square) * (1.0 / 6.0))
        factor_ref[...] = weights_ref[...] * (factor_ref[...] - xc_scale * root)

        def clear(e, carry):
            sums_ref[e] = jnp.zeros((block, block), f32)
            return carry

        lax.fori_loop(0, entries, clear, 0)

    def group(turn, carry):
        for u in range(unroll):
            s = turn * unroll + u
            basis = basis_ref[s]
            scaled = (basis.astype(f32) * factor_ref[pl.ds(start + s, 1), :]).astype(bf16)
            full = lax.dot_general(
                basis, scaled, (((1,), (1,)), ((), ())), preferred_element_type=f32
            )
            for k in range(LIST):
                for l in range(LIST):
                    e = pairs_ref[(start + s) * LIST * LIST + k * LIST + l]
                    sums_ref[e] += full[
                        k * block : (k + 1) * block, l * block : (l + 1) * block
                    ]
        return carry

    lax.fori_loop(0, slots // unroll, group, 0)

    @pl.when(start == total - slots)
    def _():
        low = lax.broadcasted_iota(jnp.int32, (1, 8, block), 1) < 4
        for c in range(out_ref.shape[2]):
            first = sums_ref[2 * c].reshape(block // 8, 8, block)
            second = sums_ref[2 * c + 1].reshape(block // 8, 8, block)
            out_ref[:, 0, c] = jnp.where(low, first, pltpu.roll(second, 4, 1)).astype(bf16)
            out_ref[:, 1, c] = jnp.where(low, pltpu.roll(first, 4, 1), second).astype(bf16)


def add_kernel(target_ref, received_ref, out_ref):
    rows = out_ref.shape[1]
    length = target_ref.shape[1]
    chosen = lax.broadcasted_iota(jnp.int32, (rows, length), 0) == target_ref[...]
    total = jnp.dot(
        chosen.astype(f32).astype(bf16), received_ref[...], preferred_element_type=f32
    ).astype(bf16)
    for h in range(out_ref.shape[0]):
        out_ref[h] = total


def place_kernel(spread_ref, plan_ref, rank_ref, density_ref):
    slots = density_ref.shape[0]
    length = plan_ref.shape[1]
    own = lax.broadcasted_iota(jnp.int32, (slots, length), 0) + rank_ref[0] * slots
    chosen = (own == plan_ref[...]).astype(f32).astype(bf16)
    density_ref[...] = jnp.dot(chosen, spread_ref[...], preferred_element_type=f32)


def merge_kernel(received_ref, out_ref):
    half, _, rows, block = received_ref.shape
    low = lax.broadcasted_iota(jnp.int32, (1, 8, block), 1) < 4
    for at in range(0, rows, 16):
        even = received_ref[:, 0, at : at + 16, :].astype(f32)
        odd = received_ref[:, 1, at : at + 16, :].astype(f32)
        for q in range(2):
            first = even[:, 8 * q : 8 * q + 8]
            second = odd[:, 8 * q : 8 * q + 8]
            place = at // 4 + 2 * q
            out_ref[place] = jnp.where(low, first, pltpu.roll(second, 4, 1)).reshape(8 * half, block)
            out_ref[place + 1] = jnp.where(low, pltpu.roll(first, 4, 1), second).reshape(
                8 * half, block
            )


def to_all(value, axis):
    copies = jnp.broadcast_to(value[None], (lax.axis_size(axis),) + value.shape)
    return lax.all_to_all(copies, axis, split_axis=0, concat_axis=0, tiled=True)


def on_device(
    points,
    centers,
    exponents,
    angular,
    grid_weights,
    hartree,
    load_plan,
    density_blocks,
    pair_lists,
    batch_pairs,
):
    slots, _, _, grid = points.shape
    ranks = lax.axis_size("batch")
    columns = lax.axis_size("blk")
    per_owner = pair_lists.shape[3]
    held, block, _ = density_blocks.shape
    entries = columns * per_owner
    width = LIST * block
    piece = block // ranks
    rank = lax.axis_index("batch")
    plan_rows = lax.dynamic_slice_in_dim(load_plan[0], rank * slots, slots)

    wanted = pair_lists[0, 0]
    asked = lax.all_to_all(wanted, "blk", split_axis=0, concat_axis=0, tiled=True).reshape(entries)
    sent = call(
        pick_kernel,
        jax.ShapeDtypeStruct((entries, block, block), bf16),
        [SMEM, VMEM],
        moved=entries * block * block * 4,
    )(asked, density_blocks)
    table = lax.all_to_all(
        sent.reshape(columns, per_owner * block, block), "blk", split_axis=0, concat_axis=0, tiled=True
    ).reshape(entries, block, block)

    params = jnp.concatenate(
        [centers[:, 0], exponents, angular[:, 0], jnp.zeros((slots, 1, width), f32)], axis=1
    )
    group = min(4, slots)
    steps = (slots // group,)
    basis, done = call(
        basis_kernel,
        (jax.ShapeDtypeStruct((slots, width, grid), bf16), jax.ShapeDtypeStruct((8, block), f32)),
        [rows_of(group, 3, grid), rows_of(group, 8, width)],
        grid=steps,
        out_specs=(rows_of(group, width, grid), VMEM),
        limit=48,
        flops=slots * width * grid * 400,
        moved=slots * width * grid * 2,
    )(points[:, 0], params)

    stride = slots + 8
    stored = to_all(
        call(
            spread_kernel,
            jax.ShapeDtypeStruct((stride, grid), f32),
            [VMEM, VMEM, HBM],
        )(
            hartree[:, 0],
            jnp.pad(asked.reshape(1, entries).astype(f32), ((0, 0), (0, grid - entries))),
            done,
        ),
        "batch",
    ).reshape(ranks * stride, grid)

    pairs = batch_pairs.reshape(slots * LIST * LIST)
    unroll = 2
    rho = call(
        density_kernel,
        jax.ShapeDtypeStruct((slots, grid), f32),
        [SMEM, rows_of(group, width, grid), VMEM],
        [pltpu.VMEM((unroll, width, width), bf16)],
        grid=steps,
        limit=48,
        flops=slots * width * width * grid * 2,
        moved=slots * width * grid * 2,
    )(pairs, basis, table)
    spread = to_all(rho.astype(bf16), "batch").reshape(ranks * slots, grid)
    partial, lists = call(
        matrix_kernel,
        (
            jax.ShapeDtypeStruct((ranks // 2, 2, columns, per_owner * piece, block), bf16),
            jax.ShapeDtypeStruct((ranks, block), f32),
        ),
        [SMEM, SMEM, rows_of(group, width, grid), VMEM, VMEM, VMEM],
        [pltpu.VMEM((entries, block, block), f32), pltpu.VMEM((slots, grid), f32)],
        grid=steps,
        limit=48,
        flops=slots * width * width * grid * 2,
        moved=slots * width * grid * 2,
    )(pairs, plan_rows, basis, rho, stored, grid_weights[:, 0])

    rows = per_owner * piece
    partial, spread = lax.optimization_barrier((partial, spread))
    received = lax.all_to_all(
        partial.reshape(ranks * columns, rows, block),
        ("batch", "blk"),
        split_axis=0,
        concat_axis=0,
        tiled=True,
    ).reshape(ranks * columns * rows, block)
    density = call(
        place_kernel,
        jax.ShapeDtypeStruct((slots, grid), f32),
        [VMEM, VMEM, SMEM],
        moved=ranks * slots * grid * 2,
    )(spread, load_plan, rank.reshape(1))

    targets = lists[:, :entries].astype(jnp.int32).reshape(ranks * entries, 1) * piece
    targets = (targets + jnp.arange(piece, dtype=jnp.int32)[None]).reshape(
        1, ranks * entries * piece
    )
    totals = call(
        add_kernel,
        jax.ShapeDtypeStruct((ranks, held * piece, block), bf16),
        [VMEM, VMEM],
        moved=ranks * columns * rows * block * 2,
    )(targets, received)
    gathered = lax.all_to_all(totals, "batch", split_axis=0, concat_axis=0, tiled=True)
    hamiltonian = call(
        merge_kernel,
        jax.ShapeDtypeStruct((held, block, block), f32),
        [VMEM],
        moved=held * block * block * 6,
    )(gathered.reshape(ranks // 2, 2, held * piece, block))
    return (hamiltonian, density[:, None, :])


def solution(mesh):
    return jax.shard_map(
        on_device,
        mesh=mesh,
        in_specs=(
            P("batch", "blk", None, None),
            P("batch", "blk", None, None),
            P("batch", "blk", None),
            P("batch", "blk", None, None),
            P("batch", "blk", None),
            P("batch", "blk", None),
            P("blk", None),
            P("blk", None, None),
            P("batch", "blk", None, None),
            P("batch", "blk", None),
        ),
        out_specs=(P("blk", None, None), P("batch", "blk", None)),
        check_vma=False,
    )
```

```python
import jax
import jax.numpy as jnp
from jax import lax
from jax.experimental import pallas as pl
from jax.experimental.pallas import tpu as pltpu
from jax.sharding import PartitionSpec as P

LIST = 3
xc_scale = 0.98474502
soft_square = 0.01
zero_exchange = xc_scale * soft_square ** (1.0 / 6.0)
log2_e = 1.4426950408889634

bf16 = jnp.bfloat16
f32 = jnp.float32
VMEM = pl.BlockSpec(memory_space=pltpu.VMEM)
HBM = pl.BlockSpec(memory_space=pltpu.HBM)
SMEM = pl.BlockSpec(memory_space=pltpu.SMEM)


def rows_of(*block):
    return pl.BlockSpec(block, lambda n: (n,) + (0,) * (len(block) - 1))


def call(body, outs, ins, scratch=(), flops=0, moved=0, limit=24, grid=(), out_specs=None):
    return pl.pallas_call(
        body,
        out_shape=outs,
        grid=grid,
        in_specs=ins,
        out_specs=out_specs or jax.tree.map(lambda _: VMEM, outs),
        scratch_shapes=list(scratch),
        compiler_params=pltpu.CompilerParams(vmem_limit_bytes=limit * 2**20),
        cost_estimate=pl.CostEstimate(flops=flops, bytes_accessed=moved, transcendentals=0),
    )


def basis_kernel(points_ref, params_ref, out_ref, done_ref):
    slots, width, _ = out_ref.shape
    step = 32
    done_ref[...] = jnp.zeros_like(done_ref)

    def one(s, carry):
        columns = jnp.transpose(params_ref[s])
        for at in range(0, width, step):
            own = columns[at : at + step]
            distance = None
            angular = None
            for a in range(3):
                delta = points_ref[s, a : a + 1, :] - own[:, a : a + 1]
                square = delta * delta
                slope = own[:, 4 + a : 5 + a] * delta
                distance = square if a == 0 else distance + square
                angular = slope + 1.0 if a == 0 else angular + slope
            value = jnp.exp2((own[:, 3:4] * -log2_e) * distance) * angular
            out_ref[s, at : at + step, :] = value.astype(bf16)
        return carry

    lax.fori_loop(0, slots, one, 0)


def pick_kernel(asked_ref, blocks_ref, out_ref):
    for e in range(out_ref.shape[0]):
        out_ref[e] = blocks_ref[asked_ref[e]]


def spread_kernel(hartree_ref, listed_ref, done_ref, out_ref):
    del done_ref
    _, rows, grid = out_ref.shape
    below = jnp.broadcast_to(listed_ref[...], (rows - hartree_ref.shape[0], grid))
    lines = jnp.concatenate([hartree_ref[...] - zero_exchange, below]).astype(bf16)
    for h in range(out_ref.shape[0]):
        out_ref[h] = lines


def density_kernel(pairs_ref, basis_ref, table_ref, rho_ref, copies_ref, sub_ref):
    slots = basis_ref.shape[0]
    block = table_ref.shape[1]
    unroll = sub_ref.shape[0]
    start = pl.program_id(0) * slots

    def group(turn, carry):
        for u in range(unroll):
            s = turn * unroll + u
            for k in range(LIST):
                for l in range(LIST):
                    sub_ref[u, k * block : (k + 1) * block, l * block : (l + 1) * block] = table_ref[
                        pairs_ref[(start + s) * LIST * LIST + k * LIST + l]
                    ]
        for u in range(unroll):
            s = turn * unroll + u
            basis = basis_ref[s]
            inner = jnp.dot(sub_ref[u], basis, preferred_element_type=f32)
            rho_ref[pl.ds(start + s, 1), :] = jnp.sum(inner * basis.astype(f32), axis=0, keepdims=True)
        return carry

    lax.fori_loop(0, slots // unroll, group, 0)

    @pl.when(start == rho_ref.shape[0] - slots)
    def _():
        sent = rho_ref[...].astype(bf16)
        for h in range(copies_ref.shape[0]):
            copies_ref[h] = sent


def matrix_kernel(
    pairs_ref, plan_ref, basis_ref, rho_ref, hartree_ref, weights_ref,
    out_ref, lists_ref, sums_ref, factor_ref, stored_ref,
):
    slots = basis_ref.shape[0]
    total = rho_ref.shape[0]
    entries, block, _ = sums_ref.shape
    stride = hartree_ref.shape[1]
    unroll = 2
    start = pl.program_id(0) * slots

    @pl.when(start == 0)
    def _():
        for r in range(lists_ref.shape[0]):
            lines = hartree_ref[r].astype(f32)
            stored_ref[r * stride : (r + 1) * stride, :] = lines
            lists_ref[r : r + 1, :] = lines[total : total + 1, :block]
        for s in range(total):
            at = plan_ref[s]
            factor_ref[s : s + 1, :] = stored_ref[
                pl.ds(lax.div(at, total) * stride + lax.rem(at, total), 1), :
            ]
        rho = rho_ref[...]
        root = jnp.exp2(jnp.log2(rho * rho + soft_square) * (1.0 / 6.0))
        factor_ref[...] = weights_ref[...] * (factor_ref[...] + (zero_exchange - xc_scale * root))

        def clear(e, carry):
            sums_ref[e] = jnp.zeros((block, block), f32)
            return carry

        lax.fori_loop(0, entries, clear, 0)

    def group(turn, carry):
        for u in range(unroll):
            s = turn * unroll + u
            basis = basis_ref[s]
            scaled = (basis.astype(f32) * factor_ref[pl.ds(start + s, 1), :]).astype(bf16)
            full = lax.dot_general(
                basis, scaled, (((1,), (1,)), ((), ())), preferred_element_type=f32
            )
            for k in range(LIST):
                for l in range(LIST):
                    e = pairs_ref[(start + s) * LIST * LIST + k * LIST + l]
                    sums_ref[e] += full[
                        k * block : (k + 1) * block, l * block : (l + 1) * block
                    ]
        return carry

    lax.fori_loop(0, slots // unroll, group, 0)

    @pl.when(start == total - slots)
    def _():
        low = lax.broadcasted_iota(jnp.int32, (1, 8, block), 1) < 4
        for c in range(out_ref.shape[2]):
            first = sums_ref[2 * c].reshape(block // 8, 8, block)
            second = sums_ref[2 * c + 1].reshape(block // 8, 8, block)
            out_ref[:, 0, c] = jnp.where(low, first, pltpu.roll(second, 4, 1)).astype(bf16)
            out_ref[:, 1, c] = jnp.where(low, pltpu.roll(first, 4, 1), second).astype(bf16)


def add_kernel(target_ref, received_ref, out_ref):
    rows = out_ref.shape[1]
    length = target_ref.shape[1]
    chosen = lax.broadcasted_iota(jnp.int32, (rows, length), 0) == target_ref[...]
    total = jnp.dot(
        chosen.astype(f32).astype(bf16), received_ref[...], preferred_element_type=f32
    ).astype(bf16)
    for h in range(out_ref.shape[0]):
        out_ref[h] = total


def place_kernel(spread_ref, plan_ref, rank_ref, density_ref):
    slots = density_ref.shape[0]
    length = plan_ref.shape[1]
    own = lax.broadcasted_iota(jnp.int32, (slots, length), 0) + rank_ref[0] * slots
    chosen = (own == plan_ref[...]).astype(f32).astype(bf16)
    density_ref[...] = jnp.dot(chosen, spread_ref[...], preferred_element_type=f32)


def merge_kernel(received_ref, out_ref):
    half, _, rows, block = received_ref.shape
    low = lax.broadcasted_iota(jnp.int32, (1, 8, block), 1) < 4
    for at in range(0, rows, 16):
        even = received_ref[:, 0, at : at + 16, :].astype(f32)
        odd = received_ref[:, 1, at : at + 16, :].astype(f32)
        for q in range(2):
            first = even[:, 8 * q : 8 * q + 8]
            second = odd[:, 8 * q : 8 * q + 8]
            place = at // 4 + 2 * q
            out_ref[place] = jnp.where(low, first, pltpu.roll(second, 4, 1)).reshape(8 * half, block)
            out_ref[place + 1] = jnp.where(low, pltpu.roll(first, 4, 1), second).reshape(
                8 * half, block
            )


def on_device(
    points,
    centers,
    exponents,
    angular,
    grid_weights,
    hartree,
    load_plan,
    density_blocks,
    pair_lists,
    batch_pairs,
):
    slots, _, _, grid = points.shape
    ranks = lax.axis_size("batch")
    columns = lax.axis_size("blk")
    per_owner = pair_lists.shape[3]
    held, block, _ = density_blocks.shape
    entries = columns * per_owner
    width = LIST * block
    piece = block // ranks
    rank = lax.axis_index("batch")
    plan_rows = lax.dynamic_slice_in_dim(load_plan[0], rank * slots, slots)

    wanted = pair_lists[0, 0]
    asked = lax.all_to_all(wanted, "blk", split_axis=0, concat_axis=0, tiled=True).reshape(entries)
    sent = call(
        pick_kernel,
        jax.ShapeDtypeStruct((entries, block, block), bf16),
        [SMEM, VMEM],
        moved=entries * block * block * 4,
    )(asked, density_blocks)
    table = lax.all_to_all(
        sent.reshape(columns, per_owner * block, block), "blk", split_axis=0, concat_axis=0, tiled=True
    ).reshape(entries, block, block)

    params = jnp.concatenate(
        [centers[:, 0], exponents, angular[:, 0], jnp.zeros((slots, 1, width), f32)], axis=1
    )
    group = min(4, slots)
    steps = (slots // group,)
    basis, done = call(
        basis_kernel,
        (jax.ShapeDtypeStruct((slots, width, grid), bf16), jax.ShapeDtypeStruct((8, block), f32)),
        [rows_of(group, 3, grid), rows_of(group, 8, width)],
        grid=steps,
        out_specs=(rows_of(group, width, grid), VMEM),
        limit=48,
        flops=slots * width * grid * 400,
        moved=slots * width * grid * 2,
    )(points[:, 0], params)

    stride = slots + 8
    lines = call(
        spread_kernel,
        jax.ShapeDtypeStruct((ranks, stride, grid), bf16),
        [VMEM, VMEM, HBM],
    )(
        hartree[:, 0],
        jnp.pad(asked.reshape(1, entries).astype(f32), ((0, 0), (0, grid - entries))),
        done,
    )
    stored = lax.all_to_all(lines, "batch", split_axis=0, concat_axis=0, tiled=True)

    pairs = batch_pairs.reshape(slots * LIST * LIST)
    unroll = 2
    rho, copies = call(
        density_kernel,
        (
            jax.ShapeDtypeStruct((slots, grid), f32),
            jax.ShapeDtypeStruct((ranks, slots, grid), bf16),
        ),
        [SMEM, rows_of(group, width, grid), VMEM],
        [pltpu.VMEM((unroll, width, width), bf16)],
        grid=steps,
        limit=48,
        flops=slots * width * width * grid * 2,
        moved=slots * width * grid * 2,
    )(pairs, basis, table)
    spread = lax.all_to_all(copies, "batch", split_axis=0, concat_axis=0, tiled=True).reshape(
        ranks * slots, grid
    )
    partial, lists = call(
        matrix_kernel,
        (
            jax.ShapeDtypeStruct((ranks // 2, 2, columns, per_owner * piece, block), bf16),
            jax.ShapeDtypeStruct((ranks, block), f32),
        ),
        [SMEM, SMEM, rows_of(group, width, grid), VMEM, VMEM, VMEM],
        [
            pltpu.VMEM((entries, block, block), f32),
            pltpu.VMEM((slots, grid), f32),
            pltpu.VMEM((ranks * stride, grid), f32),
        ],
        grid=steps,
        limit=48,
        flops=slots * width * width * grid * 2,
        moved=slots * width * grid * 2,
    )(pairs, plan_rows, basis, rho, stored, grid_weights[:, 0])

    rows = per_owner * piece
    partial, spread = lax.optimization_barrier((partial, spread))
    received = lax.all_to_all(
        partial.reshape(ranks * columns, rows, block),
        ("batch", "blk"),
        split_axis=0,
        concat_axis=0,
        tiled=True,
    ).reshape(ranks * columns * rows, block)
    density = call(
        place_kernel,
        jax.ShapeDtypeStruct((slots, grid), f32),
        [VMEM, VMEM, SMEM],
        moved=ranks * slots * grid * 2,
    )(spread, load_plan, rank.reshape(1))

    targets = lists[:, :entries].astype(jnp.int32).reshape(ranks * entries, 1) * piece
    targets = (targets + jnp.arange(piece, dtype=jnp.int32)[None]).reshape(
        1, ranks * entries * piece
    )
    totals = call(
        add_kernel,
        jax.ShapeDtypeStruct((ranks, held * piece, block), bf16),
        [VMEM, VMEM],
        moved=ranks * columns * rows * block * 2,
    )(targets, received)
    gathered = lax.all_to_all(totals, "batch", split_axis=0, concat_axis=0, tiled=True)
    hamiltonian = call(
        merge_kernel,
        jax.ShapeDtypeStruct((held, block, block), f32),
        [VMEM],
        moved=held * block * block * 6,
    )(gathered.reshape(ranks // 2, 2, held * piece, block))
    return (hamiltonian, density[:, None, :])


def solution(mesh):
    return jax.shard_map(
        on_device,
        mesh=mesh,
        in_specs=(
            P("batch", "blk", None, None),
            P("batch", "blk", None, None),
            P("batch", "blk", None),
            P("batch", "blk", None, None),
            P("batch", "blk", None),
            P("batch", "blk", None),
            P("blk", None),
            P("blk", None, None),
            P("batch", "blk", None, None),
            P("batch", "blk", None),
        ),
        out_specs=(P("blk", None, None), P("batch", "blk", None)),
        check_vma=False,
    )
```

```python
import jax
import jax.numpy as jnp
from jax import lax
from jax.experimental import pallas as pl
from jax.experimental.pallas import tpu as pltpu
from jax.sharding import PartitionSpec as P

LIST = 3
xc_scale = 0.98474502
soft_square = 0.01
zero_exchange = xc_scale * soft_square ** (1.0 / 6.0)
log2_e = 1.4426950408889634

bf16 = jnp.bfloat16
f32 = jnp.float32
VMEM = pl.BlockSpec(memory_space=pltpu.VMEM)
HBM = pl.BlockSpec(memory_space=pltpu.HBM)
SMEM = pl.BlockSpec(memory_space=pltpu.SMEM)


def rows_of(*block):
    return pl.BlockSpec(block, lambda n: (n,) + (0,) * (len(block) - 1))


def call(body, outs, ins, scratch=(), flops=0, moved=0, limit=24, grid=(), out_specs=None):
    return pl.pallas_call(
        body,
        out_shape=outs,
        grid=grid,
        in_specs=ins,
        out_specs=out_specs or jax.tree.map(lambda _: VMEM, outs),
        scratch_shapes=list(scratch),
        compiler_params=pltpu.CompilerParams(vmem_limit_bytes=limit * 2**20),
        cost_estimate=pl.CostEstimate(flops=flops, bytes_accessed=moved, transcendentals=0),
    )


def in_parts(value):
    high = value.astype(bf16).astype(f32)
    rest = value - high
    middle = rest.astype(bf16).astype(f32)
    return high, middle, rest - middle


LEFT = (0, 1, 2, 0, 1, 0)
RIGHT = (0, 0, 0, 1, 1, 2)
TERMS = 32


def basis_kernel(
    points_ref, centers_ref, exponents_ref, angular_ref, out_ref, done_ref, left_ref, right_ref
):
    slots = out_ref.shape[0]
    chunks, total, lanes = left_ref.shape
    total //= TERMS
    chunks //= 2
    halves = right_ref.shape[0]

    @pl.when(pl.program_id(0) == 0)
    def _():
        done_ref[...] = jnp.zeros_like(done_ref)
        none = jnp.zeros((total, lanes), f32)

        def put(ref, at, row, value):
            ref[at, pl.ds(row, total, TERMS), :] = value

        for j in range(chunks):
            scale = exponents_ref[pl.ds(j, total, chunks), :] * -log2_e
            center, slope = [], []
            for a in range(3):
                center.append(centers_ref[pl.ds(a * chunks + j, total, 3 * chunks), :])
                slope.append(angular_ref[pl.ds(a * chunks + j, total, 3 * chunks), :])
            square = center[0] * center[0] + center[1] * center[1] + center[2] * center[2]
            offset = slope[0] * center[0] + slope[1] * center[1] + slope[2] * center[2]
            logarithm = [scale] + [(-2.0 * scale) * c for c in center] + [scale * square]
            factor = [None] + slope + [1.0 - offset]
            for at, values in ((j, logarithm), (chunks + j, factor)):
                for n in range(5):
                    parts = (none, none, none) if values[n] is None else in_parts(values[n])
                    for i in range(6 if n < 4 else 3):
                        put(left_ref, at, 6 * n + i, parts[LEFT[i]])
                for row in range(27, TERMS):
                    put(left_ref, at, row, none)
        for j in range(halves):
            point = [points_ref[pl.ds(a * halves + j, total, 3 * halves), :] for a in range(3)]
            square = point[0] * point[0] + point[1] * point[1] + point[2] * point[2]
            for n, value in enumerate([square] + point):
                parts = in_parts(value)
                for i in range(6):
                    put(right_ref, j, 6 * n + i, parts[RIGHT[i]])
            for row in range(24, TERMS):
                put(right_ref, j, row, none + 1.0 if row < 27 else none)

    start = pl.program_id(0) * slots
    for s in range(slots):
        rows = pl.ds((start + s) * TERMS, TERMS)
        right = jnp.concatenate([right_ref[j, rows, :] for j in range(halves)], axis=1).astype(bf16)
        for j in range(chunks):
            found = [
                lax.dot_general(
                    left_ref[at, rows, :].astype(bf16),
                    right,
                    (((0,), (0,)), ((), ())),
                    preferred_element_type=f32,
                )
                for at in (j, chunks + j)
            ]
            value = jnp.exp2(found[0]) * found[1]
            out_ref[s, j * lanes : (j + 1) * lanes, :] = value.astype(bf16)


def pick_kernel(asked_ref, blocks_ref, out_ref, sems):
    per_owner = asked_ref.shape[2]
    copies = []
    for e in range(out_ref.shape[0]):
        place = asked_ref[e // per_owner, 0, e % per_owner]
        copies.append(pltpu.make_async_copy(blocks_ref.at[place], out_ref.at[e], sems.at[e]))
    for copy in copies:
        copy.start()
    for copy in copies:
        copy.wait()


def spread_kernel(hartree_ref, listed_ref, done_ref, out_ref):
    del done_ref
    _, rows, grid = out_ref.shape
    below = jnp.broadcast_to(listed_ref[...], (rows - hartree_ref.shape[0], grid))
    lines = jnp.concatenate([hartree_ref[...] - zero_exchange, below]).astype(bf16)
    for h in range(out_ref.shape[0]):
        out_ref[h] = lines


def density_kernel(pairs_ref, basis_ref, table_ref, rho_ref, copies_ref, sub_ref):
    slots = basis_ref.shape[0]
    block = table_ref.shape[1]
    unroll = sub_ref.shape[0]
    start = pl.program_id(0) * slots

    def group(turn, carry):
        for u in range(unroll):
            s = turn * unroll + u
            for k in range(LIST):
                for l in range(LIST):
                    sub_ref[u, k * block : (k + 1) * block, l * block : (l + 1) * block] = table_ref[
                        pairs_ref[(start + s) * LIST * LIST + k * LIST + l]
                    ]
        for u in range(unroll):
            s = turn * unroll + u
            basis = basis_ref[s]
            inner = jnp.dot(sub_ref[u], basis, preferred_element_type=f32)
            rho_ref[pl.ds(start + s, 1), :] = jnp.sum(inner * basis.astype(f32), axis=0, keepdims=True)
        return carry

    lax.fori_loop(0, slots // unroll, group, 0)

    @pl.when(start == rho_ref.shape[0] - slots)
    def _():
        sent = rho_ref[...].astype(bf16)
        for h in range(copies_ref.shape[0]):
            copies_ref[h] = sent


def matrix_kernel(
    pairs_ref, plan_ref, basis_ref, rho_ref, hartree_ref, weights_ref,
    out_ref, lists_ref, sums_ref, factor_ref, stored_ref,
):
    slots = basis_ref.shape[0]
    total = rho_ref.shape[0]
    entries, block, _ = sums_ref.shape
    stride = hartree_ref.shape[1]
    unroll = 2
    start = pl.program_id(0) * slots

    @pl.when(start == 0)
    def _():
        for r in range(lists_ref.shape[0]):
            lines = hartree_ref[r].astype(f32)
            stored_ref[r * stride : (r + 1) * stride, :] = lines
            lists_ref[r : r + 1, :] = lines[total : total + 1, :block]
        for s in range(total):
            at = plan_ref[s]
            factor_ref[s : s + 1, :] = stored_ref[
                pl.ds(lax.div(at, total) * stride + lax.rem(at, total), 1), :
            ]
        rho = rho_ref[...]
        root = jnp.exp2(jnp.log2(rho * rho + soft_square) * (1.0 / 6.0))
        factor_ref[...] = weights_ref[...] * (factor_ref[...] + (zero_exchange - xc_scale * root))

        def clear(e, carry):
            sums_ref[e] = jnp.zeros((block, block), f32)
            return carry

        lax.fori_loop(0, entries, clear, 0)

    def group(turn, carry):
        for u in range(unroll):
            s = turn * unroll + u
            basis = basis_ref[s]
            scaled = (basis.astype(f32) * factor_ref[pl.ds(start + s, 1), :]).astype(bf16)
            full = lax.dot_general(
                basis, scaled, (((1,), (1,)), ((), ())), preferred_element_type=f32
            )
            for k in range(LIST):
                for l in range(LIST):
                    e = pairs_ref[(start + s) * LIST * LIST + k * LIST + l]
                    sums_ref[e] += full[
                        k * block : (k + 1) * block, l * block : (l + 1) * block
                    ]
        return carry

    lax.fori_loop(0, slots // unroll, group, 0)

    @pl.when(start == total - slots)
    def _():
        low = lax.broadcasted_iota(jnp.int32, (1, 8, block), 1) < 4
        for c in range(out_ref.shape[2]):
            first = sums_ref[2 * c].reshape(block // 8, 8, block)
            second = sums_ref[2 * c + 1].reshape(block // 8, 8, block)
            out_ref[:, 0, c] = jnp.where(low, first, pltpu.roll(second, 4, 1)).astype(bf16)
            out_ref[:, 1, c] = jnp.where(low, pltpu.roll(first, 4, 1), second).astype(bf16)


def add_kernel(target_ref, received_ref, out_ref):
    rows = out_ref.shape[1]
    length = target_ref.shape[1]
    chosen = lax.broadcasted_iota(jnp.int32, (rows, length), 0) == target_ref[...]
    total = jnp.dot(
        chosen.astype(f32).astype(bf16), received_ref[...], preferred_element_type=f32
    ).astype(bf16)
    for h in range(out_ref.shape[0]):
        out_ref[h] = total


def place_kernel(spread_ref, plan_ref, rank_ref, density_ref):
    slots = density_ref.shape[0]
    length = plan_ref.shape[1]
    own = lax.broadcasted_iota(jnp.int32, (slots, length), 0) + rank_ref[0] * slots
    chosen = (own == plan_ref[...]).astype(f32).astype(bf16)
    density_ref[...] = jnp.dot(chosen, spread_ref[...], preferred_element_type=f32)


def merge_kernel(received_ref, out_ref):
    half, _, rows, block = received_ref.shape
    low = lax.broadcasted_iota(jnp.int32, (1, 8, block), 1) < 4
    for at in range(0, rows, 16):
        even = received_ref[:, 0, at : at + 16, :].astype(f32)
        odd = received_ref[:, 1, at : at + 16, :].astype(f32)
        for q in range(2):
            first = even[:, 8 * q : 8 * q + 8]
            second = odd[:, 8 * q : 8 * q + 8]
            place = at // 4 + 2 * q
            out_ref[place] = jnp.where(low, first, pltpu.roll(second, 4, 1)).reshape(8 * half, block)
            out_ref[place + 1] = jnp.where(low, pltpu.roll(first, 4, 1), second).reshape(
                8 * half, block
            )


def on_device(
    points,
    centers,
    exponents,
    angular,
    grid_weights,
    hartree,
    load_plan,
    density_blocks,
    pair_lists,
    batch_pairs,
):
    slots, _, _, grid = points.shape
    ranks = lax.axis_size("batch")
    columns = lax.axis_size("blk")
    per_owner = pair_lists.shape[3]
    held, block, _ = density_blocks.shape
    entries = columns * per_owner
    width = LIST * block
    piece = block // ranks
    rank = lax.axis_index("batch")
    plan_rows = lax.dynamic_slice_in_dim(load_plan[0], rank * slots, slots)

    wanted = pair_lists.reshape(columns, 1, per_owner)
    asked = lax.all_to_all(wanted, "blk", split_axis=0, concat_axis=0, tiled=True)
    sent = call(
        pick_kernel,
        jax.ShapeDtypeStruct((entries, block, block), bf16),
        [SMEM, HBM],
        [pltpu.SemaphoreType.DMA((entries,))],
        out_specs=HBM,
        limit=60,
        moved=entries * block * block * 4,
    )(asked, density_blocks)
    table = lax.all_to_all(
        sent.reshape(columns, per_owner * block, block), "blk", split_axis=0, concat_axis=0, tiled=True
    ).reshape(entries, block, block)

    group = min(4, slots)
    steps = (slots // group,)
    basis, done = call(
        basis_kernel,
        (jax.ShapeDtypeStruct((slots, width, grid), bf16), jax.ShapeDtypeStruct((8, block), f32)),
        [VMEM, VMEM, VMEM, VMEM],
        [
            pltpu.VMEM((2 * LIST, slots * TERMS, block), f32),
            pltpu.VMEM((grid // block, slots * TERMS, block), f32),
        ],
        grid=steps,
        out_specs=(rows_of(group, width, grid), VMEM),
        limit=48,
        flops=slots * width * grid * 400,
        moved=slots * width * grid * 2,
    )(
        points.reshape(-1, block),
        centers.reshape(-1, block),
        exponents.reshape(-1, block),
        angular.reshape(-1, block),
    )

    stride = slots + 8
    lines = call(
        spread_kernel,
        jax.ShapeDtypeStruct((ranks, stride, grid), bf16),
        [VMEM, VMEM, HBM],
    )(
        hartree[:, 0],
        jnp.pad(asked.reshape(1, entries).astype(f32), ((0, 0), (0, grid - entries))),
        done,
    )
    stored = lax.all_to_all(lines, "batch", split_axis=0, concat_axis=0, tiled=True)

    pairs = batch_pairs.reshape(slots * LIST * LIST)
    unroll = 2
    rho, copies = call(
        density_kernel,
        (
            jax.ShapeDtypeStruct((slots, grid), f32),
            jax.ShapeDtypeStruct((ranks, slots, grid), bf16),
        ),
        [SMEM, rows_of(group, width, grid), VMEM],
        [pltpu.VMEM((unroll, width, width), bf16)],
        grid=steps,
        limit=48,
        flops=slots * width * width * grid * 2,
        moved=slots * width * grid * 2,
    )(pairs, basis, table)
    spread = lax.all_to_all(copies, "batch", split_axis=0, concat_axis=0, tiled=True).reshape(
        ranks * slots, grid
    )
    partial, lists = call(
        matrix_kernel,
        (
            jax.ShapeDtypeStruct((ranks // 2, 2, columns, per_owner * piece, block), bf16),
            jax.ShapeDtypeStruct((ranks, block), f32),
        ),
        [SMEM, SMEM, rows_of(group, width, grid), VMEM, VMEM, VMEM],
        [
            pltpu.VMEM((entries, block, block), f32),
            pltpu.VMEM((slots, grid), f32),
            pltpu.VMEM((ranks * stride, grid), f32),
        ],
        grid=steps,
        limit=48,
        flops=slots * width * width * grid * 2,
        moved=slots * width * grid * 2,
    )(pairs, plan_rows, basis, rho, stored, grid_weights[:, 0])

    rows = per_owner * piece
    partial, spread = lax.optimization_barrier((partial, spread))
    received = lax.all_to_all(
        partial.reshape(ranks * columns, rows, block),
        ("batch", "blk"),
        split_axis=0,
        concat_axis=0,
        tiled=True,
    ).reshape(ranks * columns * rows, block)
    density = call(
        place_kernel,
        jax.ShapeDtypeStruct((slots, grid), f32),
        [VMEM, VMEM, SMEM],
        moved=ranks * slots * grid * 2,
    )(spread, load_plan, rank.reshape(1))

    targets = lists[:, :entries].astype(jnp.int32).reshape(ranks * entries, 1) * piece
    targets = (targets + jnp.arange(piece, dtype=jnp.int32)[None]).reshape(
        1, ranks * entries * piece
    )
    totals = call(
        add_kernel,
        jax.ShapeDtypeStruct((ranks, held * piece, block), bf16),
        [VMEM, VMEM],
        moved=ranks * columns * rows * block * 2,
    )(targets, received)
    gathered = lax.all_to_all(totals, "batch", split_axis=0, concat_axis=0, tiled=True)
    hamiltonian = call(
        merge_kernel,
        jax.ShapeDtypeStruct((held, block, block), f32),
        [VMEM],
        moved=held * block * block * 6,
    )(gathered.reshape(ranks // 2, 2, held * piece, block))
    return (hamiltonian, density[:, None, :])


def solution(mesh):
    return jax.shard_map(
        on_device,
        mesh=mesh,
        in_specs=(
            P("batch", "blk", None, None),
            P("batch", "blk", None, None),
            P("batch", "blk", None),
            P("batch", "blk", None, None),
            P("batch", "blk", None),
            P("batch", "blk", None),
            P("blk", None),
            P("blk", None, None),
            P("batch", "blk", None, None),
            P("batch", "blk", None),
        ),
        out_specs=(P("blk", None, None), P("batch", "blk", None)),
        check_vma=False,
    )
```

```python
import jax
import jax.numpy as jnp
from jax import lax
from jax.experimental import pallas as pl
from jax.experimental.pallas import tpu as pltpu
from jax.sharding import PartitionSpec as P

LIST = 3
BATCH = ("z", "x")
xc_scale = 0.98474502
soft_square = 0.01
zero_exchange = xc_scale * soft_square ** (1.0 / 6.0)
log2_e = 1.4426950408889634

bf16 = jnp.bfloat16
f32 = jnp.float32
VMEM = pl.BlockSpec(memory_space=pltpu.VMEM)
HBM = pl.BlockSpec(memory_space=pltpu.HBM)
SMEM = pl.BlockSpec(memory_space=pltpu.SMEM)


def rows_of(*block):
    return pl.BlockSpec(block, lambda n: (n,) + (0,) * (len(block) - 1))


def call(body, outs, ins, scratch=(), flops=0, moved=0, limit=24, grid=(), out_specs=None):
    return pl.pallas_call(
        body,
        out_shape=outs,
        grid=grid,
        in_specs=ins,
        out_specs=out_specs or jax.tree.map(lambda _: VMEM, outs),
        scratch_shapes=list(scratch),
        compiler_params=pltpu.CompilerParams(vmem_limit_bytes=limit * 2**20),
        cost_estimate=pl.CostEstimate(flops=flops, bytes_accessed=moved, transcendentals=0),
    )


def in_parts(value):
    high = value.astype(bf16).astype(f32)
    rest = value - high
    middle = rest.astype(bf16).astype(f32)
    return high, middle, rest - middle


LEFT = (0, 1, 2, 0, 1, 0)
RIGHT = (0, 0, 0, 1, 1, 2)
TERMS = 32


def basis_kernel(
    points_ref, centers_ref, exponents_ref, angular_ref, out_ref, done_ref, left_ref, right_ref
):
    slots = out_ref.shape[0]
    chunks, total, lanes = left_ref.shape
    total //= TERMS
    chunks //= 2
    halves = right_ref.shape[0]

    @pl.when(pl.program_id(0) == 0)
    def _():
        done_ref[...] = jnp.zeros_like(done_ref)
        none = jnp.zeros((total, lanes), f32)

        def put(ref, at, row, value):
            ref[at, pl.ds(row, total, TERMS), :] = value

        for j in range(chunks):
            scale = exponents_ref[pl.ds(j, total, chunks), :] * -log2_e
            center, slope = [], []
            for a in range(3):
                center.append(centers_ref[pl.ds(a * chunks + j, total, 3 * chunks), :])
                slope.append(angular_ref[pl.ds(a * chunks + j, total, 3 * chunks), :])
            square = center[0] * center[0] + center[1] * center[1] + center[2] * center[2]
            offset = slope[0] * center[0] + slope[1] * center[1] + slope[2] * center[2]
            logarithm = [scale] + [(-2.0 * scale) * c for c in center] + [scale * square]
            factor = [None] + slope + [1.0 - offset]
            for at, values in ((j, logarithm), (chunks + j, factor)):
                for n in range(5):
                    parts = (none, none, none) if values[n] is None else in_parts(values[n])
                    for i in range(6 if n < 4 else 3):
                        put(left_ref, at, 6 * n + i, parts[LEFT[i]])
                for row in range(27, TERMS):
                    put(left_ref, at, row, none)
        for j in range(halves):
            point = [points_ref[pl.ds(a * halves + j, total, 3 * halves), :] for a in range(3)]
            square = point[0] * point[0] + point[1] * point[1] + point[2] * point[2]
            for n, value in enumerate([square] + point):
                parts = in_parts(value)
                for i in range(6):
                    put(right_ref, j, 6 * n + i, parts[RIGHT[i]])
            for row in range(24, TERMS):
                put(right_ref, j, row, none + 1.0 if row < 27 else none)

    start = pl.program_id(0) * slots
    for s in range(slots):
        rows = pl.ds((start + s) * TERMS, TERMS)
        right = jnp.concatenate([right_ref[j, rows, :] for j in range(halves)], axis=1).astype(bf16)
        for j in range(chunks):
            found = [
                lax.dot_general(
                    left_ref[at, rows, :].astype(bf16),
                    right,
                    (((0,), (0,)), ((), ())),
                    preferred_element_type=f32,
                )
                for at in (j, chunks + j)
            ]
            value = jnp.exp2(found[0]) * found[1]
            out_ref[s, j * lanes : (j + 1) * lanes, :] = value.astype(bf16)


def pick_kernel(asked_ref, blocks_ref, out_ref):
    per_owner = asked_ref.shape[2]
    for e in range(out_ref.shape[0]):
        out_ref[e] = blocks_ref[asked_ref[e // per_owner, 0, e % per_owner]]


def spread_kernel(hartree_ref, listed_ref, done_ref, out_ref):
    del done_ref
    _, rows, grid = out_ref.shape
    below = jnp.broadcast_to(listed_ref[...], (rows - hartree_ref.shape[0], grid))
    lines = jnp.concatenate([hartree_ref[...] - zero_exchange, below]).astype(bf16)
    for h in range(out_ref.shape[0]):
        out_ref[h] = lines


def density_kernel(pairs_ref, basis_ref, table_ref, rho_ref, copies_ref, sub_ref):
    slots = basis_ref.shape[0]
    block = table_ref.shape[1]
    unroll = sub_ref.shape[0]
    start = pl.program_id(0) * slots

    def group(turn, carry):
        for u in range(unroll):
            s = turn * unroll + u
            for k in range(LIST):
                for l in range(LIST):
                    sub_ref[u, k * block : (k + 1) * block, l * block : (l + 1) * block] = table_ref[
                        pairs_ref[(start + s) * LIST * LIST + k * LIST + l]
                    ]
        for u in range(unroll):
            s = turn * unroll + u
            basis = basis_ref[s]
            inner = jnp.dot(sub_ref[u], basis, preferred_element_type=f32)
            rho_ref[pl.ds(start + s, 1), :] = jnp.sum(inner * basis.astype(f32), axis=0, keepdims=True)
        return carry

    lax.fori_loop(0, slots // unroll, group, 0)

    @pl.when(start == rho_ref.shape[0] - slots)
    def _():
        sent = rho_ref[...].astype(bf16)
        for h in range(copies_ref.shape[0]):
            copies_ref[h] = sent


def matrix_kernel(
    pairs_ref, plan_ref, basis_ref, rho_ref, hartree_ref, weights_ref,
    out_ref, lists_ref, sums_ref, factor_ref, stored_ref,
):
    slots = basis_ref.shape[0]
    total = rho_ref.shape[0]
    entries, block, _ = sums_ref.shape
    stride = hartree_ref.shape[1]
    unroll = 2
    start = pl.program_id(0) * slots

    @pl.when(start == 0)
    def _():
        for r in range(lists_ref.shape[0]):
            lines = hartree_ref[r].astype(f32)
            stored_ref[r * stride : (r + 1) * stride, :] = lines
            lists_ref[r : r + 1, :] = lines[total : total + 1, :block]
        for s in range(total):
            at = plan_ref[s]
            factor_ref[s : s + 1, :] = stored_ref[
                pl.ds(lax.div(at, total) * stride + lax.rem(at, total), 1), :
            ]
        rho = rho_ref[...]
        root = jnp.exp2(jnp.log2(rho * rho + soft_square) * (1.0 / 6.0))
        factor_ref[...] = weights_ref[...] * (factor_ref[...] + (zero_exchange - xc_scale * root))

        def clear(e, carry):
            sums_ref[e] = jnp.zeros((block, block), f32)
            return carry

        lax.fori_loop(0, entries, clear, 0)

    def group(turn, carry):
        for u in range(unroll):
            s = turn * unroll + u
            basis = basis_ref[s]
            scaled = (basis.astype(f32) * factor_ref[pl.ds(start + s, 1), :]).astype(bf16)
            full = lax.dot_general(
                basis, scaled, (((1,), (1,)), ((), ())), preferred_element_type=f32
            )
            for k in range(LIST):
                for l in range(LIST):
                    e = pairs_ref[(start + s) * LIST * LIST + k * LIST + l]
                    sums_ref[e] += full[
                        k * block : (k + 1) * block, l * block : (l + 1) * block
                    ]
        return carry

    lax.fori_loop(0, slots // unroll, group, 0)

    @pl.when(start == total - slots)
    def _():
        low = lax.broadcasted_iota(jnp.int32, (1, 8, block), 1) < 4
        for c in range(out_ref.shape[2]):
            first = sums_ref[2 * c].reshape(block // 8, 8, block)
            second = sums_ref[2 * c + 1].reshape(block // 8, 8, block)
            out_ref[:, 0, c] = jnp.where(low, first, pltpu.roll(second, 4, 1)).astype(bf16)
            out_ref[:, 1, c] = jnp.where(low, pltpu.roll(first, 4, 1), second).astype(bf16)


def add_kernel(target_ref, received_ref, density_ref, out_ref):
    del density_ref
    rows = out_ref.shape[1]
    length = target_ref.shape[1]
    chosen = lax.broadcasted_iota(jnp.int32, (rows, length), 0) == target_ref[...]
    total = jnp.dot(
        chosen.astype(f32).astype(bf16), received_ref[...], preferred_element_type=f32
    ).astype(bf16)
    for h in range(out_ref.shape[0]):
        out_ref[h] = total


def place_kernel(plan_ref, place_ref, *refs):
    density_ref = refs[-1]
    slots = density_ref.shape[0]
    planes, length = plan_ref.shape
    own = lax.broadcasted_iota(jnp.int32, (slots, length), 0) + place_ref[1] * slots
    total = jnp.zeros(density_ref.shape, f32)
    for k in range(planes):
        plane = lax.rem(place_ref[0] + (planes - k), planes)
        chosen = (own == plan_ref[pl.ds(plane, 1), :]).astype(f32).astype(bf16)
        total += jnp.dot(chosen, refs[k][...], preferred_element_type=f32)
    density_ref[...] = total


def merge_kernel(received_ref, out_ref):
    half, _, rows, block = received_ref.shape
    low = lax.broadcasted_iota(jnp.int32, (1, 8, block), 1) < 4
    for at in range(0, rows, 16):
        even = received_ref[:, 0, at : at + 16, :].astype(f32)
        odd = received_ref[:, 1, at : at + 16, :].astype(f32)
        for q in range(2):
            first = even[:, 8 * q : 8 * q + 8]
            second = odd[:, 8 * q : 8 * q + 8]
            place = at // 4 + 2 * q
            out_ref[place] = jnp.where(low, first, pltpu.roll(second, 4, 1)).reshape(8 * half, block)
            out_ref[place + 1] = jnp.where(low, pltpu.roll(first, 4, 1), second).reshape(
                8 * half, block
            )


def on_device(
    points,
    centers,
    exponents,
    angular,
    grid_weights,
    hartree,
    load_plan,
    density_blocks,
    pair_lists,
    batch_pairs,
):
    slots, _, _, grid = points.shape
    ranks = lax.axis_size(BATCH)
    columns = lax.axis_size("blk")
    per_owner = pair_lists.shape[3]
    held, block, _ = density_blocks.shape
    entries = columns * per_owner
    width = LIST * block
    piece = block // ranks
    rank = lax.axis_index(BATCH)
    plan_rows = lax.dynamic_slice_in_dim(load_plan[0], rank * slots, slots)

    wanted = pair_lists.reshape(columns, 1, per_owner)
    asked = lax.all_to_all(wanted, "blk", split_axis=0, concat_axis=0, tiled=True)
    sent = call(
        pick_kernel,
        jax.ShapeDtypeStruct((entries, block, block), bf16),
        [SMEM, VMEM],
        moved=entries * block * block * 4,
    )(asked, density_blocks)
    table = lax.all_to_all(
        sent.reshape(columns, per_owner * block, block), "blk", split_axis=0, concat_axis=0, tiled=True
    ).reshape(entries, block, block)

    group = min(4, slots)
    steps = (slots // group,)
    basis, done = call(
        basis_kernel,
        (jax.ShapeDtypeStruct((slots, width, grid), bf16), jax.ShapeDtypeStruct((8, block), f32)),
        [VMEM, VMEM, VMEM, VMEM],
        [
            pltpu.VMEM((2 * LIST, slots * TERMS, block), f32),
            pltpu.VMEM((grid // block, slots * TERMS, block), f32),
        ],
        grid=steps,
        out_specs=(rows_of(group, width, grid), VMEM),
        limit=48,
        flops=slots * width * grid * 400,
        moved=slots * width * grid * 2,
    )(
        points.reshape(-1, block),
        centers.reshape(-1, block),
        exponents.reshape(-1, block),
        angular.reshape(-1, block),
    )

    stride = slots + 8
    lines = call(
        spread_kernel,
        jax.ShapeDtypeStruct((ranks, stride, grid), bf16),
        [VMEM, VMEM, HBM],
    )(
        hartree[:, 0],
        jnp.pad(asked.reshape(1, entries).astype(f32), ((0, 0), (0, grid - entries))),
        done,
    )
    stored = lax.all_to_all(lines, BATCH, split_axis=0, concat_axis=0, tiled=True)

    pairs = batch_pairs.reshape(slots * LIST * LIST)
    unroll = 2
    rho, copies = call(
        density_kernel,
        (
            jax.ShapeDtypeStruct((slots, grid), f32),
            jax.ShapeDtypeStruct((lax.axis_size("x"), slots, grid), bf16),
        ),
        [SMEM, rows_of(group, width, grid), VMEM],
        [pltpu.VMEM((unroll, width, width), bf16)],
        grid=steps,
        limit=48,
        flops=slots * width * width * grid * 2,
        moved=slots * width * grid * 2,
    )(pairs, basis, table)
    near = lax.all_to_all(copies, "x", split_axis=0, concat_axis=0, tiled=True).reshape(-1, grid)
    partial, lists = call(
        matrix_kernel,
        (
            jax.ShapeDtypeStruct((ranks // 2, 2, columns, per_owner * piece, block), bf16),
            jax.ShapeDtypeStruct((ranks, block), f32),
        ),
        [SMEM, SMEM, rows_of(group, width, grid), VMEM, VMEM, VMEM],
        [
            pltpu.VMEM((entries, block, block), f32),
            pltpu.VMEM((slots, grid), f32),
            pltpu.VMEM((ranks * stride, grid), f32),
        ],
        grid=steps,
        limit=48,
        flops=slots * width * width * grid * 2,
        moved=slots * width * grid * 2,
    )(pairs, plan_rows, basis, rho, stored, grid_weights[:, 0])

    rows = per_owner * piece
    partial, near = lax.optimization_barrier((partial, near))
    received = lax.all_to_all(
        partial.reshape(ranks * columns, rows, block),
        BATCH + ("blk",),
        split_axis=0,
        concat_axis=0,
        tiled=True,
    ).reshape(ranks * columns * rows, block)
    planes = lax.axis_size("z")
    spread = [near] + [
        lax.ppermute(near, "z", [(n, (n + k) % planes) for n in range(planes)])
        for k in range(1, planes)
    ]
    density = call(
        place_kernel,
        jax.ShapeDtypeStruct((slots, grid), f32),
        [VMEM, SMEM] + [VMEM] * planes,
        moved=ranks * slots * grid * 2,
    )(load_plan.reshape(planes, -1), jnp.stack([lax.axis_index("z"), rank]), *spread)

    targets = lists[:, :entries].astype(jnp.int32).reshape(ranks * entries, 1) * piece
    targets = (targets + jnp.arange(piece, dtype=jnp.int32)[None]).reshape(
        1, ranks * entries * piece
    )
    totals = call(
        add_kernel,
        jax.ShapeDtypeStruct((ranks, held * piece, block), bf16),
        [VMEM, VMEM, HBM],
        moved=ranks * columns * rows * block * 2,
    )(targets, received, density)
    gathered = lax.all_to_all(totals, BATCH, split_axis=0, concat_axis=0, tiled=True)
    hamiltonian = call(
        merge_kernel,
        jax.ShapeDtypeStruct((held, block, block), f32),
        [VMEM],
        moved=held * block * block * 6,
    )(gathered.reshape(ranks // 2, 2, held * piece, block))
    return (hamiltonian, density[:, None, :])


def solution(mesh):
    ranks, columns = mesh.devices.shape
    fine = jax.sharding.Mesh(mesh.devices.reshape(ranks // 4, 4, columns), BATCH + ("blk",))
    return jax.shard_map(
        on_device,
        mesh=fine,
        in_specs=(
            P(BATCH, "blk", None, None),
            P(BATCH, "blk", None, None),
            P(BATCH, "blk", None),
            P(BATCH, "blk", None, None),
            P(BATCH, "blk", None),
            P(BATCH, "blk", None),
            P("blk", None),
            P("blk", None, None),
            P(BATCH, "blk", None, None),
            P(BATCH, "blk", None),
        ),
        out_specs=(P("blk", None, None), P(BATCH, "blk", None)),
        check_vma=False,
    )
```

```python
import functools

import jax
import jax.numpy as jnp
from jax import lax
from jax.experimental import pallas as pl
from jax.experimental.pallas import tpu as pltpu
from jax.sharding import PartitionSpec as P

LIST = 3
BATCH = ("z", "x")
xc_scale = 0.98474502
soft_square = 0.01
zero_exchange = xc_scale * soft_square ** (1.0 / 6.0)
log2_e = 1.4426950408889634

bf16 = jnp.bfloat16
f32 = jnp.float32
VMEM = pl.BlockSpec(memory_space=pltpu.VMEM)
HBM = pl.BlockSpec(memory_space=pltpu.HBM)
SMEM = pl.BlockSpec(memory_space=pltpu.SMEM)


def rows_of(*block):
    return pl.BlockSpec(block, lambda n: (n,) + (0,) * (len(block) - 1))


def call(body, outs, ins, scratch=(), flops=0, moved=0, limit=24, grid=(), out_specs=None):
    return pl.pallas_call(
        body,
        out_shape=outs,
        grid=grid,
        in_specs=ins,
        out_specs=out_specs or jax.tree.map(lambda _: VMEM, outs),
        scratch_shapes=list(scratch),
        compiler_params=pltpu.CompilerParams(vmem_limit_bytes=limit * 2**20),
        cost_estimate=pl.CostEstimate(flops=flops, bytes_accessed=moved, transcendentals=0),
    )


def in_parts(value):
    high = value.astype(bf16).astype(f32)
    rest = value - high
    middle = rest.astype(bf16).astype(f32)
    return high, middle, rest - middle


LEFT = (0, 1, 2, 0, 1, 0)
RIGHT = (0, 0, 0, 1, 1, 2)
TERMS = 32


def basis_kernel(
    points_ref, centers_ref, exponents_ref, angular_ref, out_ref, done_ref, left_ref, right_ref
):
    slots = out_ref.shape[0]
    chunks, total, lanes = left_ref.shape
    total //= TERMS
    chunks //= 2
    halves = right_ref.shape[0]

    @pl.when(pl.program_id(0) == 0)
    def _():
        done_ref[...] = jnp.zeros_like(done_ref)
        none = jnp.zeros((total, lanes), f32)

        def put(ref, at, row, value):
            ref[at, pl.ds(row, total, TERMS), :] = value

        for j in range(chunks):
            scale = exponents_ref[pl.ds(j, total, chunks), :] * -log2_e
            center, slope = [], []
            for a in range(3):
                center.append(centers_ref[pl.ds(a * chunks + j, total, 3 * chunks), :])
                slope.append(angular_ref[pl.ds(a * chunks + j, total, 3 * chunks), :])
            square = center[0] * center[0] + center[1] * center[1] + center[2] * center[2]
            offset = slope[0] * center[0] + slope[1] * center[1] + slope[2] * center[2]
            logarithm = [scale] + [(-2.0 * scale) * c for c in center] + [scale * square]
            factor = [None] + slope + [1.0 - offset]
            for at, values in ((j, logarithm), (chunks + j, factor)):
                for n in range(5):
                    parts = (none, none, none) if values[n] is None else in_parts(values[n])
                    for i in range(6 if n < 4 else 3):
                        put(left_ref, at, 6 * n + i, parts[LEFT[i]])
                for row in range(27, TERMS):
                    put(left_ref, at, row, none)
        for j in range(halves):
            point = [points_ref[pl.ds(a * halves + j, total, 3 * halves), :] for a in range(3)]
            square = point[0] * point[0] + point[1] * point[1] + point[2] * point[2]
            for n, value in enumerate([square] + point):
                parts = in_parts(value)
                for i in range(6):
                    put(right_ref, j, 6 * n + i, parts[RIGHT[i]])
            for row in range(24, TERMS):
                put(right_ref, j, row, none + 1.0 if row < 27 else none)

    start = pl.program_id(0) * slots
    for s in range(slots):
        rows = pl.ds((start + s) * TERMS, TERMS)
        right = jnp.concatenate([right_ref[j, rows, :] for j in range(halves)], axis=1).astype(bf16)
        for j in range(chunks):
            found = [
                lax.dot_general(
                    left_ref[at, rows, :].astype(bf16),
                    right,
                    (((0,), (0,)), ((), ())),
                    preferred_element_type=f32,
                )
                for at in (j, chunks + j)
            ]
            value = jnp.exp2(found[0]) * found[1]
            out_ref[s, j * lanes : (j + 1) * lanes, :] = value.astype(bf16)


def pick_kernel(asked_ref, blocks_ref, out_ref):
    per_owner = asked_ref.shape[2]
    for e in range(out_ref.shape[0]):
        out_ref[e] = blocks_ref[asked_ref[e // per_owner, 0, e % per_owner]]


def spread_kernel(hartree_ref, listed_ref, done_ref, out_ref):
    del done_ref
    _, rows, grid = out_ref.shape
    below = jnp.broadcast_to(listed_ref[...], (rows - hartree_ref.shape[0], grid))
    lines = jnp.concatenate([hartree_ref[...] - zero_exchange, below]).astype(bf16)
    for h in range(out_ref.shape[0]):
        out_ref[h] = lines


def density_kernel(pairs_ref, basis_ref, table_ref, rho_ref, copies_ref, sub_ref):
    slots = basis_ref.shape[0]
    block = table_ref.shape[1]
    unroll = sub_ref.shape[0]
    start = pl.program_id(0) * slots

    def group(turn, carry):
        for u in range(unroll):
            s = turn * unroll + u
            for k in range(LIST):
                for l in range(LIST):
                    sub_ref[u, k * block : (k + 1) * block, l * block : (l + 1) * block] = table_ref[
                        pairs_ref[(start + s) * LIST * LIST + k * LIST + l]
                    ]
        for u in range(unroll):
            s = turn * unroll + u
            basis = basis_ref[s]
            inner = jnp.dot(sub_ref[u], basis, preferred_element_type=f32)
            rho_ref[pl.ds(start + s, 1), :] = jnp.sum(inner * basis.astype(f32), axis=0, keepdims=True)
        return carry

    lax.fori_loop(0, slots // unroll, group, 0)

    @pl.when(start == rho_ref.shape[0] - slots)
    def _():
        sent = rho_ref[...].astype(bf16)
        for h in range(copies_ref.shape[0]):
            copies_ref[h] = sent


def matrix_kernel(
    pairs_ref, plan_ref, basis_ref, rho_ref, hartree_ref, weights_ref,
    out_ref, lists_ref, sums_ref, factor_ref, stored_ref,
):
    slots = basis_ref.shape[0]
    total = rho_ref.shape[0]
    entries, block, _ = sums_ref.shape
    stride = hartree_ref.shape[1]
    unroll = slots
    start = pl.program_id(0) * slots

    @pl.when(start == 0)
    def _():
        for r in range(lists_ref.shape[0]):
            lines = hartree_ref[r].astype(f32)
            stored_ref[r * stride : (r + 1) * stride, :] = lines
            lists_ref[r : r + 1, :] = lines[total : total + 1, :block]
        for s in range(total):
            at = plan_ref[s]
            factor_ref[s : s + 1, :] = stored_ref[
                pl.ds(lax.div(at, total) * stride + lax.rem(at, total), 1), :
            ]
        rho = rho_ref[...]
        root = jnp.exp2(jnp.log2(rho * rho + soft_square) * (1.0 / 6.0))
        factor_ref[...] = weights_ref[...] * (factor_ref[...] + (zero_exchange - xc_scale * root))

        def clear(e, carry):
            sums_ref[e] = jnp.zeros((block, block), f32)
            return carry

        lax.fori_loop(0, entries, clear, 0)

    def group(turn, carry):
        for u in range(unroll):
            s = turn * unroll + u
            basis = basis_ref[s]
            scaled = (basis.astype(f32) * factor_ref[pl.ds(start + s, 1), :]).astype(bf16)
            full = lax.dot_general(
                basis, scaled, (((1,), (1,)), ((), ())), preferred_element_type=f32
            )
            for k in range(LIST):
                for l in range(LIST):
                    e = pairs_ref[(start + s) * LIST * LIST + k * LIST + l]
                    sums_ref[e] += full[
                        k * block : (k + 1) * block, l * block : (l + 1) * block
                    ]
        return carry

    lax.fori_loop(0, slots // unroll, group, 0)

    @pl.when(start == total - slots)
    def _():
        low = lax.broadcasted_iota(jnp.int32, (1, 8, block), 1) < 4
        for c in range(out_ref.shape[2]):
            first = sums_ref[2 * c].reshape(block // 8, 8, block)
            second = sums_ref[2 * c + 1].reshape(block // 8, 8, block)
            out_ref[:, 0, c] = jnp.where(low, first, pltpu.roll(second, 4, 1)).astype(bf16)
            out_ref[:, 1, c] = jnp.where(low, pltpu.roll(first, 4, 1), second).astype(bf16)


def add_kernel(target_ref, received_ref, density_ref, out_ref):
    del density_ref
    rows = out_ref.shape[1]
    length = target_ref.shape[1]
    chosen = lax.broadcasted_iota(jnp.int32, (rows, length), 0) == target_ref[...]
    total = jnp.dot(
        chosen.astype(f32).astype(bf16), received_ref[...], preferred_element_type=f32
    ).astype(bf16)
    for h in range(out_ref.shape[0]):
        out_ref[h] = total


def place_kernel(first, plan_ref, place_ref, *refs):
    before_ref, density_ref = refs[0], refs[-1]
    slots = density_ref.shape[0]
    planes, length = plan_ref.shape
    own = lax.broadcasted_iota(jnp.int32, (slots, length), 0) + place_ref[1] * slots
    total = before_ref[...]
    for k, plane_ref in enumerate(refs[1:-1], first):
        plane = lax.rem(place_ref[0] + (planes - k), planes)
        chosen = (own == plan_ref[pl.ds(plane, 1), :]).astype(f32).astype(bf16)
        total += jnp.dot(chosen, plane_ref[...], preferred_element_type=f32)
    density_ref[...] = total


def merge_kernel(received_ref, out_ref):
    half, _, rows, block = received_ref.shape
    low = lax.broadcasted_iota(jnp.int32, (1, 8, block), 1) < 4
    for at in range(0, rows, 16):
        even = received_ref[:, 0, at : at + 16, :].astype(f32)
        odd = received_ref[:, 1, at : at + 16, :].astype(f32)
        for q in range(2):
            first = even[:, 8 * q : 8 * q + 8]
            second = odd[:, 8 * q : 8 * q + 8]
            place = at // 4 + 2 * q
            out_ref[place] = jnp.where(low, first, pltpu.roll(second, 4, 1)).reshape(8 * half, block)
            out_ref[place + 1] = jnp.where(low, pltpu.roll(first, 4, 1), second).reshape(
                8 * half, block
            )


def on_device(
    points,
    centers,
    exponents,
    angular,
    grid_weights,
    hartree,
    load_plan,
    density_blocks,
    pair_lists,
    batch_pairs,
):
    slots, _, _, grid = points.shape
    ranks = lax.axis_size(BATCH)
    columns = lax.axis_size("blk")
    per_owner = pair_lists.shape[3]
    held, block, _ = density_blocks.shape
    entries = columns * per_owner
    width = LIST * block
    piece = block // ranks
    rank = lax.axis_index(BATCH)
    plan_rows = lax.dynamic_slice_in_dim(load_plan[0], rank * slots, slots)

    wanted = pair_lists.reshape(columns, 1, per_owner)
    asked = lax.all_to_all(wanted, "blk", split_axis=0, concat_axis=0, tiled=True)
    sent = call(
        pick_kernel,
        jax.ShapeDtypeStruct((entries, block, block), bf16),
        [SMEM, VMEM],
        moved=entries * block * block * 4,
    )(asked, density_blocks)
    table = lax.all_to_all(
        sent.reshape(columns, per_owner * block, block), "blk", split_axis=0, concat_axis=0, tiled=True
    ).reshape(entries, block, block)

    group = min(4, slots)
    steps = (slots // group,)
    basis, done = call(
        basis_kernel,
        (jax.ShapeDtypeStruct((slots, width, grid), bf16), jax.ShapeDtypeStruct((8, block), f32)),
        [VMEM, VMEM, VMEM, VMEM],
        [
            pltpu.VMEM((2 * LIST, slots * TERMS, block), f32),
            pltpu.VMEM((grid // block, slots * TERMS, block), f32),
        ],
        grid=steps,
        out_specs=(rows_of(group, width, grid), VMEM),
        limit=48,
        flops=slots * width * grid * 400,
        moved=slots * width * grid * 2,
    )(
        points.reshape(-1, block),
        centers.reshape(-1, block),
        exponents.reshape(-1, block),
        angular.reshape(-1, block),
    )

    stride = slots + 8
    lines = call(
        spread_kernel,
        jax.ShapeDtypeStruct((ranks, stride, grid), bf16),
        [VMEM, VMEM, HBM],
    )(
        hartree[:, 0],
        jnp.pad(asked.reshape(1, entries).astype(f32), ((0, 0), (0, grid - entries))),
        done,
    )
    stored = lax.all_to_all(lines, BATCH, split_axis=0, concat_axis=0, tiled=True)

    pairs = batch_pairs.reshape(slots * LIST * LIST)
    unroll = 2
    rho, copies = call(
        density_kernel,
        (
            jax.ShapeDtypeStruct((slots, grid), f32),
            jax.ShapeDtypeStruct((lax.axis_size("x"), slots, grid), bf16),
        ),
        [SMEM, rows_of(group, width, grid), VMEM],
        [pltpu.VMEM((unroll, width, width), bf16)],
        grid=steps,
        limit=48,
        flops=slots * width * width * grid * 2,
        moved=slots * width * grid * 2,
    )(pairs, basis, table)
    near = lax.all_to_all(copies, "x", split_axis=0, concat_axis=0, tiled=True).reshape(-1, grid)
    wide = min(8, slots)
    partial, lists = call(
        matrix_kernel,
        (
            jax.ShapeDtypeStruct((ranks // 2, 2, columns, per_owner * piece, block), bf16),
            jax.ShapeDtypeStruct((ranks, block), f32),
        ),
        [SMEM, SMEM, rows_of(wide, width, grid), VMEM, VMEM, VMEM],
        [
            pltpu.VMEM((entries, block, block), f32),
            pltpu.VMEM((slots, grid), f32),
            pltpu.VMEM((ranks * stride, grid), f32),
        ],
        grid=(slots // wide,),
        limit=48,
        flops=slots * width * width * grid * 2,
        moved=slots * width * grid * 2,
    )(pairs, plan_rows, basis, rho, stored, grid_weights[:, 0])

    rows = per_owner * piece
    partial, near = lax.optimization_barrier((partial, near))
    received = lax.all_to_all(
        partial.reshape(ranks * columns, rows, block),
        BATCH + ("blk",),
        split_axis=0,
        concat_axis=0,
        tiled=True,
    ).reshape(ranks * columns * rows, block)
    planes = lax.axis_size("z")
    spread = [near] + [
        lax.ppermute(near, "z", [(n, (n + k) % planes) for n in range(planes)])
        for k in range(1, planes)
    ]
    place = jnp.stack([lax.axis_index("z"), rank])

    def placed(before, first, last):
        count = last - first
        return call(
            functools.partial(place_kernel, first),
            jax.ShapeDtypeStruct((slots, grid), f32),
            [VMEM, SMEM] + [VMEM] * (1 + count),
            moved=ranks * slots * grid * 2,
        )(load_plan.reshape(planes, -1), place, before, *spread[first:last])

    cut = planes // 2 + 1
    density = placed(jnp.zeros((slots, grid), f32), 0, cut)

    targets = lists[:, :entries].astype(jnp.int32).reshape(ranks * entries, 1) * piece
    targets = (targets + jnp.arange(piece, dtype=jnp.int32)[None]).reshape(
        1, ranks * entries * piece
    )
    totals = call(
        add_kernel,
        jax.ShapeDtypeStruct((ranks, held * piece, block), bf16),
        [VMEM, VMEM, HBM],
        moved=ranks * columns * rows * block * 2,
    )(targets, received, density)
    density = placed(density, cut, planes)
    gathered = lax.all_to_all(totals, BATCH, split_axis=0, concat_axis=0, tiled=True)
    hamiltonian = call(
        merge_kernel,
        jax.ShapeDtypeStruct((held, block, block), f32),
        [VMEM],
        moved=held * block * block * 6,
    )(gathered.reshape(ranks // 2, 2, held * piece, block))
    return (hamiltonian, density[:, None, :])


def solution(mesh):
    ranks, columns = mesh.devices.shape
    fine = jax.sharding.Mesh(mesh.devices.reshape(ranks // 4, 4, columns), BATCH + ("blk",))
    return jax.shard_map(
        on_device,
        mesh=fine,
        in_specs=(
            P(BATCH, "blk", None, None),
            P(BATCH, "blk", None, None),
            P(BATCH, "blk", None),
            P(BATCH, "blk", None, None),
            P(BATCH, "blk", None),
            P(BATCH, "blk", None),
            P("blk", None),
            P("blk", None, None),
            P(BATCH, "blk", None, None),
            P(BATCH, "blk", None),
        ),
        out_specs=(P("blk", None, None), P(BATCH, "blk", None)),
        check_vma=False,
    )
```

```python
import jax
import jax.numpy as jnp
from jax import lax
from jax.experimental import pallas as pl
from jax.experimental.pallas import tpu as pltpu
from jax.sharding import PartitionSpec as P

LIST = 3
BATCH = ("z", "x")
xc_scale = 0.98474502
soft_square = 0.01
zero_exchange = xc_scale * soft_square ** (1.0 / 6.0)
log2_e = 1.4426950408889634

bf16 = jnp.bfloat16
f32 = jnp.float32
VMEM = pl.BlockSpec(memory_space=pltpu.VMEM)
HBM = pl.BlockSpec(memory_space=pltpu.HBM)
SMEM = pl.BlockSpec(memory_space=pltpu.SMEM)


def rows_of(*block):
    return pl.BlockSpec(block, lambda n: (n,) + (0,) * (len(block) - 1))


def call(body, outs, ins, scratch=(), flops=0, moved=0, limit=24, grid=(), out_specs=None):
    return pl.pallas_call(
        body,
        out_shape=outs,
        grid=grid,
        in_specs=ins,
        out_specs=out_specs or jax.tree.map(lambda _: VMEM, outs),
        scratch_shapes=list(scratch),
        compiler_params=pltpu.CompilerParams(vmem_limit_bytes=limit * 2**20),
        cost_estimate=pl.CostEstimate(flops=flops, bytes_accessed=moved, transcendentals=0),
    )


def in_parts(value):
    high = value.astype(bf16).astype(f32)
    rest = value - high
    middle = rest.astype(bf16).astype(f32)
    return high, middle, rest - middle


LEFT = (0, 1, 2, 0, 1, 0)
RIGHT = (0, 0, 0, 1, 1, 2)
TERMS = 32


def basis_kernel(
    points_ref, centers_ref, exponents_ref, angular_ref, out_ref, done_ref, left_ref, right_ref
):
    slots = out_ref.shape[0]
    chunks, total, lanes = left_ref.shape
    total //= TERMS
    chunks //= 2
    halves = right_ref.shape[0]

    @pl.when(pl.program_id(0) == 0)
    def _():
        done_ref[...] = jnp.zeros_like(done_ref)
        none = jnp.zeros((total, lanes), f32)

        def put(ref, at, row, value):
            ref[at, pl.ds(row, total, TERMS), :] = value

        for j in range(chunks):
            scale = exponents_ref[pl.ds(j, total, chunks), :] * -log2_e
            center, slope = [], []
            for a in range(3):
                center.append(centers_ref[pl.ds(a * chunks + j, total, 3 * chunks), :])
                slope.append(angular_ref[pl.ds(a * chunks + j, total, 3 * chunks), :])
            square = center[0] * center[0] + center[1] * center[1] + center[2] * center[2]
            offset = slope[0] * center[0] + slope[1] * center[1] + slope[2] * center[2]
            logarithm = [scale] + [(-2.0 * scale) * c for c in center] + [scale * square]
            factor = [None] + slope + [1.0 - offset]
            for at, values in ((j, logarithm), (chunks + j, factor)):
                for n in range(5):
                    parts = (none, none, none) if values[n] is None else in_parts(values[n])
                    for i in range(6 if n < 4 else 3):
                        put(left_ref, at, 6 * n + i, parts[LEFT[i]])
                for row in range(27, TERMS):
                    put(left_ref, at, row, none)
        for j in range(halves):
            point = [points_ref[pl.ds(a * halves + j, total, 3 * halves), :] for a in range(3)]
            square = point[0] * point[0] + point[1] * point[1] + point[2] * point[2]
            for n, value in enumerate([square] + point):
                parts = in_parts(value)
                for i in range(6):
                    put(right_ref, j, 6 * n + i, parts[RIGHT[i]])
            for row in range(24, TERMS):
                put(right_ref, j, row, none + 1.0 if row < 27 else none)

    start = pl.program_id(0) * slots
    for s in range(slots):
        rows = pl.ds((start + s) * TERMS, TERMS)
        right = jnp.concatenate([right_ref[j, rows, :] for j in range(halves)], axis=1).astype(bf16)
        for j in range(chunks):
            found = [
                lax.dot_general(
                    left_ref[at, rows, :].astype(bf16),
                    right,
                    (((0,), (0,)), ((), ())),
                    preferred_element_type=f32,
                )
                for at in (j, chunks + j)
            ]
            value = jnp.exp2(found[0]) * found[1]
            out_ref[s, j * lanes : (j + 1) * lanes, :] = value.astype(bf16)


def pick_kernel(asked_ref, blocks_ref, out_ref):
    per_owner = asked_ref.shape[2]
    for e in range(out_ref.shape[0]):
        out_ref[e] = blocks_ref[asked_ref[e // per_owner, 0, e % per_owner]]


def spread_kernel(hartree_ref, listed_ref, done_ref, out_ref):
    del done_ref
    _, rows, grid = out_ref.shape
    below = jnp.broadcast_to(listed_ref[...], (rows - hartree_ref.shape[0], grid))
    lines = jnp.concatenate([hartree_ref[...] - zero_exchange, below]).astype(bf16)
    for h in range(out_ref.shape[0]):
        out_ref[h] = lines


def density_kernel(pairs_ref, basis_ref, table_ref, rho_ref, copies_ref, sub_ref):
    slots = basis_ref.shape[0]
    block = table_ref.shape[1]
    unroll = sub_ref.shape[0]
    start = pl.program_id(0) * slots

    def group(turn, carry):
        for u in range(unroll):
            s = turn * unroll + u
            for k in range(LIST):
                for l in range(LIST):
                    sub_ref[u, k * block : (k + 1) * block, l * block : (l + 1) * block] = table_ref[
                        pairs_ref[(start + s) * LIST * LIST + k * LIST + l]
                    ]
        for u in range(unroll):
            s = turn * unroll + u
            basis = basis_ref[s]
            inner = jnp.dot(sub_ref[u], basis, preferred_element_type=f32)
            rho_ref[pl.ds(start + s, 1), :] = jnp.sum(inner * basis.astype(f32), axis=0, keepdims=True)
        return carry

    lax.fori_loop(0, slots // unroll, group, 0)

    @pl.when(start == rho_ref.shape[0] - slots)
    def _():
        sent = rho_ref[...].astype(bf16)
        for h in range(copies_ref.shape[0]):
            copies_ref[h] = sent


def matrix_kernel(
    pairs_ref, plan_ref, basis_ref, rho_ref, hartree_ref, weights_ref,
    out_ref, lists_ref, sums_ref, factor_ref, stored_ref,
):
    slots = basis_ref.shape[0]
    total = rho_ref.shape[0]
    entries, block, _ = sums_ref.shape
    stride = hartree_ref.shape[1]
    unroll = slots
    start = pl.program_id(0) * slots

    @pl.when(start == 0)
    def _():
        for r in range(lists_ref.shape[0]):
            lines = hartree_ref[r].astype(f32)
            stored_ref[r * stride : (r + 1) * stride, :] = lines
            lists_ref[r : r + 1, :] = lines[total : total + 1, :block]
        for s in range(total):
            at = plan_ref[s]
            factor_ref[s : s + 1, :] = stored_ref[
                pl.ds(lax.div(at, total) * stride + lax.rem(at, total), 1), :
            ]
        rho = rho_ref[...]
        root = jnp.exp2(jnp.log2(rho * rho + soft_square) * (1.0 / 6.0))
        factor_ref[...] = weights_ref[...] * (factor_ref[...] + (zero_exchange - xc_scale * root))

        def clear(e, carry):
            sums_ref[e] = jnp.zeros((block, block), f32)
            return carry

        lax.fori_loop(0, entries, clear, 0)

    def group(turn, carry):
        for u in range(unroll):
            s = turn * unroll + u
            basis = basis_ref[s]
            scaled = (basis.astype(f32) * factor_ref[pl.ds(start + s, 1), :]).astype(bf16)
            full = lax.dot_general(
                basis, scaled, (((1,), (1,)), ((), ())), preferred_element_type=f32
            )
            for k in range(LIST):
                for l in range(LIST):
                    e = pairs_ref[(start + s) * LIST * LIST + k * LIST + l]
                    sums_ref[e] += full[
                        k * block : (k + 1) * block, l * block : (l + 1) * block
                    ]
        return carry

    lax.fori_loop(0, slots // unroll, group, 0)

    @pl.when(start == total - slots)
    def _():
        low = lax.broadcasted_iota(jnp.int32, (1, 8, block), 1) < 4
        for c in range(out_ref.shape[2]):
            first = sums_ref[2 * c].reshape(block // 8, 8, block)
            second = sums_ref[2 * c + 1].reshape(block // 8, 8, block)
            out_ref[:, 0, c] = jnp.where(low, first, pltpu.roll(second, 4, 1)).astype(bf16)
            out_ref[:, 1, c] = jnp.where(low, pltpu.roll(first, 4, 1), second).astype(bf16)


def add_kernel(target_ref, received_ref, density_ref, out_ref):
    del density_ref
    rows = out_ref.shape[1]
    length = target_ref.shape[1]
    chosen = lax.broadcasted_iota(jnp.int32, (rows, length), 0) == target_ref[...]
    total = jnp.dot(
        chosen.astype(f32).astype(bf16), received_ref[...], preferred_element_type=f32
    ).astype(bf16)
    for h in range(out_ref.shape[0]):
        out_ref[h] = total


def place_kernel(spread_ref, plan_ref, rank_ref, density_ref):
    slots = density_ref.shape[0]
    length = plan_ref.shape[1]
    own = lax.broadcasted_iota(jnp.int32, (slots, length), 0) + rank_ref[0] * slots
    chosen = (own == plan_ref[...]).astype(f32).astype(bf16)
    density_ref[...] = jnp.dot(chosen, spread_ref[...], preferred_element_type=f32)


def merge_kernel(received_ref, out_ref):
    half, _, rows, block = received_ref.shape
    low = lax.broadcasted_iota(jnp.int32, (1, 8, block), 1) < 4
    for at in range(0, rows, 16):
        even = received_ref[:, 0, at : at + 16, :].astype(f32)
        odd = received_ref[:, 1, at : at + 16, :].astype(f32)
        for q in range(2):
            first = even[:, 8 * q : 8 * q + 8]
            second = odd[:, 8 * q : 8 * q + 8]
            place = at // 4 + 2 * q
            out_ref[place] = jnp.where(low, first, pltpu.roll(second, 4, 1)).reshape(8 * half, block)
            out_ref[place + 1] = jnp.where(low, pltpu.roll(first, 4, 1), second).reshape(
                8 * half, block
            )


def on_device(
    points,
    centers,
    exponents,
    angular,
    grid_weights,
    hartree,
    load_plan,
    density_blocks,
    pair_lists,
    batch_pairs,
):
    slots, _, _, grid = points.shape
    ranks = lax.axis_size(BATCH)
    columns = lax.axis_size("blk")
    per_owner = pair_lists.shape[3]
    held, block, _ = density_blocks.shape
    entries = columns * per_owner
    width = LIST * block
    piece = block // ranks
    rank = lax.axis_index(BATCH)
    plan_rows = lax.dynamic_slice_in_dim(load_plan[0], rank * slots, slots)

    wanted = pair_lists.reshape(columns, 1, per_owner)
    asked = lax.all_to_all(wanted, "blk", split_axis=0, concat_axis=0, tiled=True)
    sent = call(
        pick_kernel,
        jax.ShapeDtypeStruct((entries, block, block), bf16),
        [SMEM, VMEM],
        moved=entries * block * block * 4,
    )(asked, density_blocks)
    table = lax.all_to_all(
        sent.reshape(columns, per_owner * block, block), "blk", split_axis=0, concat_axis=0, tiled=True
    ).reshape(entries, block, block)

    group = min(4, slots)
    steps = (slots // group,)
    basis, done = call(
        basis_kernel,
        (jax.ShapeDtypeStruct((slots, width, grid), bf16), jax.ShapeDtypeStruct((8, block), f32)),
        [VMEM, VMEM, VMEM, VMEM],
        [
            pltpu.VMEM((2 * LIST, slots * TERMS, block), f32),
            pltpu.VMEM((grid // block, slots * TERMS, block), f32),
        ],
        grid=steps,
        out_specs=(rows_of(group, width, grid), VMEM),
        limit=48,
        flops=slots * width * grid * 400,
        moved=slots * width * grid * 2,
    )(
        points.reshape(-1, block),
        centers.reshape(-1, block),
        exponents.reshape(-1, block),
        angular.reshape(-1, block),
    )

    stride = slots + 8
    lines = call(
        spread_kernel,
        jax.ShapeDtypeStruct((ranks, stride, grid), bf16),
        [VMEM, VMEM, HBM],
    )(
        hartree[:, 0],
        jnp.pad(asked.reshape(1, entries).astype(f32), ((0, 0), (0, grid - entries))),
        done,
    )
    stored = lax.all_to_all(lines, BATCH, split_axis=0, concat_axis=0, tiled=True)

    pairs = batch_pairs.reshape(slots * LIST * LIST)
    unroll = 2
    rho, copies = call(
        density_kernel,
        (
            jax.ShapeDtypeStruct((slots, grid), f32),
            jax.ShapeDtypeStruct((lax.axis_size("x"), slots, grid), bf16),
        ),
        [SMEM, rows_of(group, width, grid), VMEM],
        [pltpu.VMEM((unroll, width, width), bf16)],
        grid=steps,
        limit=48,
        flops=slots * width * width * grid * 2,
        moved=slots * width * grid * 2,
    )(pairs, basis, table)
    near = lax.all_to_all(copies, "x", split_axis=0, concat_axis=0, tiled=True).reshape(-1, grid)
    wide = min(8, slots)
    partial, lists = call(
        matrix_kernel,
        (
            jax.ShapeDtypeStruct((ranks // 2, 2, columns, per_owner * piece, block), bf16),
            jax.ShapeDtypeStruct((ranks, block), f32),
        ),
        [SMEM, SMEM, rows_of(wide, width, grid), VMEM, VMEM, VMEM],
        [
            pltpu.VMEM((entries, block, block), f32),
            pltpu.VMEM((slots, grid), f32),
            pltpu.VMEM((ranks * stride, grid), f32),
        ],
        grid=(slots // wide,),
        limit=48,
        flops=slots * width * width * grid * 2,
        moved=slots * width * grid * 2,
    )(pairs, plan_rows, basis, rho, stored, grid_weights[:, 0])

    rows = per_owner * piece
    partial, near = lax.optimization_barrier((partial, near))
    received = lax.all_to_all(
        partial.reshape(ranks * columns, rows, block),
        BATCH + ("blk",),
        split_axis=0,
        concat_axis=0,
        tiled=True,
    ).reshape(ranks * columns * rows, block)
    spread = lax.all_gather(near, "z", axis=0, tiled=True)
    density = call(
        place_kernel,
        jax.ShapeDtypeStruct((slots, grid), f32),
        [VMEM, VMEM, SMEM],
        moved=ranks * slots * grid * 2,
    )(spread, load_plan, rank.reshape(1))

    targets = lists[:, :entries].astype(jnp.int32).reshape(ranks * entries, 1) * piece
    targets = (targets + jnp.arange(piece, dtype=jnp.int32)[None]).reshape(
        1, ranks * entries * piece
    )
    totals = call(
        add_kernel,
        jax.ShapeDtypeStruct((ranks, held * piece, block), bf16),
        [VMEM, VMEM, HBM],
        moved=ranks * columns * rows * block * 2,
    )(targets, received, density)
    gathered = lax.all_to_all(totals, BATCH, split_axis=0, concat_axis=0, tiled=True)
    hamiltonian = call(
        merge_kernel,
        jax.ShapeDtypeStruct((held, block, block), f32),
        [VMEM],
        moved=held * block * block * 6,
    )(gathered.reshape(ranks // 2, 2, held * piece, block))
    return (hamiltonian, density[:, None, :])


def solution(mesh):
    ranks, columns = mesh.devices.shape
    fine = jax.sharding.Mesh(mesh.devices.reshape(ranks // 4, 4, columns), BATCH + ("blk",))
    return jax.shard_map(
        on_device,
        mesh=fine,
        in_specs=(
            P(BATCH, "blk", None, None),
            P(BATCH, "blk", None, None),
            P(BATCH, "blk", None),
            P(BATCH, "blk", None, None),
            P(BATCH, "blk", None),
            P(BATCH, "blk", None),
            P("blk", None),
            P("blk", None, None),
            P(BATCH, "blk", None, None),
            P(BATCH, "blk", None),
        ),
        out_specs=(P("blk", None, None), P(BATCH, "blk", None)),
        check_vma=False,
    )
```

```python
import jax
import jax.numpy as jnp
from jax import lax
from jax.experimental import pallas as pl
from jax.experimental.pallas import tpu as pltpu
from jax.sharding import PartitionSpec as P

LIST = 3
xc_scale = 0.98474502
soft_square = 0.01
zero_exchange = xc_scale * soft_square ** (1.0 / 6.0)
log2_e = 1.4426950408889634

bf16 = jnp.bfloat16
f32 = jnp.float32
VMEM = pl.BlockSpec(memory_space=pltpu.VMEM)
HBM = pl.BlockSpec(memory_space=pltpu.HBM)
SMEM = pl.BlockSpec(memory_space=pltpu.SMEM)


def rows_of(*block):
    return pl.BlockSpec(block, lambda n: (n,) + (0,) * (len(block) - 1))


def call(body, outs, ins, scratch=(), flops=0, moved=0, limit=24, grid=(), out_specs=None):
    return pl.pallas_call(
        body,
        out_shape=outs,
        grid=grid,
        in_specs=ins,
        out_specs=out_specs or jax.tree.map(lambda _: VMEM, outs),
        scratch_shapes=list(scratch),
        compiler_params=pltpu.CompilerParams(vmem_limit_bytes=limit * 2**20),
        cost_estimate=pl.CostEstimate(flops=flops, bytes_accessed=moved, transcendentals=0),
    )


def in_parts(value):
    high = value.astype(bf16).astype(f32)
    rest = value - high
    middle = rest.astype(bf16).astype(f32)
    return high, middle, rest - middle


LEFT = (0, 1, 2, 0, 1, 0)
RIGHT = (0, 0, 0, 1, 1, 2)
TERMS = 32


def basis_kernel(
    points_ref, centers_ref, exponents_ref, angular_ref, out_ref, done_ref, left_ref, right_ref
):
    slots = out_ref.shape[0]
    chunks, total, lanes = left_ref.shape
    total //= TERMS
    chunks //= 2
    halves = right_ref.shape[0]

    @pl.when(pl.program_id(0) == 0)
    def _():
        done_ref[...] = jnp.zeros_like(done_ref)
        none = jnp.zeros((total, lanes), f32)

        def put(ref, at, row, value):
            ref[at, pl.ds(row, total, TERMS), :] = value

        for j in range(chunks):
            scale = exponents_ref[pl.ds(j, total, chunks), :] * -log2_e
            center, slope = [], []
            for a in range(3):
                center.append(centers_ref[pl.ds(a * chunks + j, total, 3 * chunks), :])
                slope.append(angular_ref[pl.ds(a * chunks + j, total, 3 * chunks), :])
            square = center[0] * center[0] + center[1] * center[1] + center[2] * center[2]
            offset = slope[0] * center[0] + slope[1] * center[1] + slope[2] * center[2]
            logarithm = [scale] + [(-2.0 * scale) * c for c in center] + [scale * square]
            factor = [None] + slope + [1.0 - offset]
            for at, values in ((j, logarithm), (chunks + j, factor)):
                for n in range(5):
                    parts = (none, none, none) if values[n] is None else in_parts(values[n])
                    for i in range(6 if n < 4 else 3):
                        put(left_ref, at, 6 * n + i, parts[LEFT[i]])
                for row in range(27, TERMS):
                    put(left_ref, at, row, none)
        for j in range(halves):
            point = [points_ref[pl.ds(a * halves + j, total, 3 * halves), :] for a in range(3)]
            square = point[0] * point[0] + point[1] * point[1] + point[2] * point[2]
            for n, value in enumerate([square] + point):
                parts = in_parts(value)
                for i in range(6):
                    put(right_ref, j, 6 * n + i, parts[RIGHT[i]])
            for row in range(24, TERMS):
                put(right_ref, j, row, none + 1.0 if row < 27 else none)

    start = pl.program_id(0) * slots
    for s in range(slots):
        rows = pl.ds((start + s) * TERMS, TERMS)
        right = jnp.concatenate([right_ref[j, rows, :] for j in range(halves)], axis=1).astype(bf16)
        for j in range(chunks):
            found = [
                lax.dot_general(
                    left_ref[at, rows, :].astype(bf16),
                    right,
                    (((0,), (0,)), ((), ())),
                    preferred_element_type=f32,
                )
                for at in (j, chunks + j)
            ]
            value = jnp.exp2(found[0]) * found[1]
            out_ref[s, j * lanes : (j + 1) * lanes, :] = value.astype(bf16)


def pick_kernel(asked_ref, blocks_ref, out_ref):
    per_owner = asked_ref.shape[2]
    for e in range(out_ref.shape[0]):
        out_ref[e] = blocks_ref[asked_ref[e // per_owner, 0, e % per_owner]]


def spread_kernel(hartree_ref, listed_ref, done_ref, out_ref):
    del done_ref
    _, rows, grid = out_ref.shape
    below = jnp.broadcast_to(listed_ref[...], (rows - hartree_ref.shape[0], grid))
    lines = jnp.concatenate([hartree_ref[...] - zero_exchange, below]).astype(bf16)
    for h in range(out_ref.shape[0]):
        out_ref[h] = lines


def density_kernel(pairs_ref, basis_ref, table_ref, rho_ref, copies_ref, sub_ref):
    slots = basis_ref.shape[0]
    block = table_ref.shape[1]
    unroll = sub_ref.shape[0]
    start = pl.program_id(0) * slots

    def group(turn, carry):
        for u in range(unroll):
            s = turn * unroll + u
            for k in range(LIST):
                for l in range(LIST):
                    sub_ref[u, k * block : (k + 1) * block, l * block : (l + 1) * block] = table_ref[
                        pairs_ref[(start + s) * LIST * LIST + k * LIST + l]
                    ]
        for u in range(unroll):
            s = turn * unroll + u
            basis = basis_ref[s]
            inner = jnp.dot(sub_ref[u], basis, preferred_element_type=f32)
            rho_ref[pl.ds(start + s, 1), :] = jnp.sum(inner * basis.astype(f32), axis=0, keepdims=True)
        return carry

    lax.fori_loop(0, slots // unroll, group, 0)

    @pl.when(start == rho_ref.shape[0] - slots)
    def _():
        sent = rho_ref[...].astype(bf16)
        for h in range(copies_ref.shape[0]):
            copies_ref[h] = sent


def matrix_kernel(
    pairs_ref, plan_ref, basis_ref, rho_ref, hartree_ref, weights_ref,
    out_ref, lists_ref, sums_ref, factor_ref, stored_ref,
):
    slots = basis_ref.shape[0]
    total = rho_ref.shape[0]
    entries, block, _ = sums_ref.shape
    stride = hartree_ref.shape[1]
    unroll = slots
    start = pl.program_id(0) * slots

    @pl.when(start == 0)
    def _():
        for r in range(lists_ref.shape[0]):
            lines = hartree_ref[r].astype(f32)
            stored_ref[r * stride : (r + 1) * stride, :] = lines
            lists_ref[r : r + 1, :] = lines[total : total + 1, :block]
        for s in range(total):
            at = plan_ref[s]
            factor_ref[s : s + 1, :] = stored_ref[
                pl.ds(lax.div(at, total) * stride + lax.rem(at, total), 1), :
            ]
        rho = rho_ref[...]
        root = jnp.exp2(jnp.log2(rho * rho + soft_square) * (1.0 / 6.0))
        factor_ref[...] = weights_ref[...] * (factor_ref[...] + (zero_exchange - xc_scale * root))

        def clear(e, carry):
            sums_ref[e] = jnp.zeros((block, block), f32)
            return carry

        lax.fori_loop(0, entries, clear, 0)

    def group(turn, carry):
        for u in range(unroll):
            s = turn * unroll + u
            basis = basis_ref[s]
            scaled = (basis.astype(f32) * factor_ref[pl.ds(start + s, 1), :]).astype(bf16)
            full = lax.dot_general(
                basis, scaled, (((1,), (1,)), ((), ())), preferred_element_type=f32
            )
            for k in range(LIST):
                for l in range(LIST):
                    e = pairs_ref[(start + s) * LIST * LIST + k * LIST + l]
                    sums_ref[e] += full[
                        k * block : (k + 1) * block, l * block : (l + 1) * block
                    ]
        return carry

    lax.fori_loop(0, slots // unroll, group, 0)

    @pl.when(start == total - slots)
    def _():
        low = lax.broadcasted_iota(jnp.int32, (1, 8, block), 1) < 4
        for c in range(out_ref.shape[2]):
            first = sums_ref[2 * c].reshape(block // 8, 8, block)
            second = sums_ref[2 * c + 1].reshape(block // 8, 8, block)
            out_ref[:, 0, c] = jnp.where(low, first, pltpu.roll(second, 4, 1)).astype(bf16)
            out_ref[:, 1, c] = jnp.where(low, pltpu.roll(first, 4, 1), second).astype(bf16)


def add_kernel(target_ref, received_ref, out_ref):
    rows = out_ref.shape[1]
    length = target_ref.shape[1]
    chosen = lax.broadcasted_iota(jnp.int32, (rows, length), 0) == target_ref[...]
    total = jnp.dot(
        chosen.astype(f32).astype(bf16), received_ref[...], preferred_element_type=f32
    ).astype(bf16)
    for h in range(out_ref.shape[0]):
        out_ref[h] = total


def place_kernel(spread_ref, plan_ref, rank_ref, density_ref):
    slots = density_ref.shape[0]
    length = plan_ref.shape[1]
    own = lax.broadcasted_iota(jnp.int32, (slots, length), 0) + rank_ref[0] * slots
    chosen = (own == plan_ref[...]).astype(f32).astype(bf16)
    density_ref[...] = jnp.dot(chosen, spread_ref[...], preferred_element_type=f32)


def merge_kernel(received_ref, out_ref):
    half, _, rows, block = received_ref.shape
    low = lax.broadcasted_iota(jnp.int32, (1, 8, block), 1) < 4
    for at in range(0, rows, 16):
        even = received_ref[:, 0, at : at + 16, :].astype(f32)
        odd = received_ref[:, 1, at : at + 16, :].astype(f32)
        for q in range(2):
            first = even[:, 8 * q : 8 * q + 8]
            second = odd[:, 8 * q : 8 * q + 8]
            place = at // 4 + 2 * q
            out_ref[place] = jnp.where(low, first, pltpu.roll(second, 4, 1)).reshape(8 * half, block)
            out_ref[place + 1] = jnp.where(low, pltpu.roll(first, 4, 1), second).reshape(
                8 * half, block
            )


def on_device(
    points,
    centers,
    exponents,
    angular,
    grid_weights,
    hartree,
    load_plan,
    density_blocks,
    pair_lists,
    batch_pairs,
):
    slots, _, _, grid = points.shape
    ranks = lax.axis_size("batch")
    columns = lax.axis_size("blk")
    per_owner = pair_lists.shape[3]
    held, block, _ = density_blocks.shape
    entries = columns * per_owner
    width = LIST * block
    piece = block // ranks
    rank = lax.axis_index("batch")
    plan_rows = lax.dynamic_slice_in_dim(load_plan[0], rank * slots, slots)

    wanted = pair_lists.reshape(columns, 1, per_owner)
    asked = lax.all_to_all(wanted, "blk", split_axis=0, concat_axis=0, tiled=True)
    sent = call(
        pick_kernel,
        jax.ShapeDtypeStruct((entries, block, block), bf16),
        [SMEM, VMEM],
        moved=entries * block * block * 4,
    )(asked, density_blocks)
    table = lax.all_to_all(
        sent.reshape(columns, per_owner * block, block), "blk", split_axis=0, concat_axis=0, tiled=True
    ).reshape(entries, block, block)

    group = min(4, slots)
    steps = (slots // group,)
    basis, done = call(
        basis_kernel,
        (jax.ShapeDtypeStruct((slots, width, grid), bf16), jax.ShapeDtypeStruct((8, block), f32)),
        [VMEM, VMEM, VMEM, VMEM],
        [
            pltpu.VMEM((2 * LIST, slots * TERMS, block), f32),
            pltpu.VMEM((grid // block, slots * TERMS, block), f32),
        ],
        grid=steps,
        out_specs=(rows_of(group, width, grid), VMEM),
        limit=48,
        flops=slots * width * grid * 400,
        moved=slots * width * grid * 2,
    )(
        points.reshape(-1, block),
        centers.reshape(-1, block),
        exponents.reshape(-1, block),
        angular.reshape(-1, block),
    )

    stride = slots + 8
    lines = call(
        spread_kernel,
        jax.ShapeDtypeStruct((ranks, stride, grid), bf16),
        [VMEM, VMEM, HBM],
    )(
        hartree[:, 0],
        jnp.pad(asked.reshape(1, entries).astype(f32), ((0, 0), (0, grid - entries))),
        done,
    )
    stored = lax.all_to_all(lines, "batch", split_axis=0, concat_axis=0, tiled=True)

    pairs = batch_pairs.reshape(slots * LIST * LIST)
    unroll = 2
    rho, copies = call(
        density_kernel,
        (
            jax.ShapeDtypeStruct((slots, grid), f32),
            jax.ShapeDtypeStruct((ranks, slots, grid), bf16),
        ),
        [SMEM, rows_of(group, width, grid), VMEM],
        [pltpu.VMEM((unroll, width, width), bf16)],
        grid=steps,
        limit=48,
        flops=slots * width * width * grid * 2,
        moved=slots * width * grid * 2,
    )(pairs, basis, table)
    spread = lax.all_to_all(copies, "batch", split_axis=0, concat_axis=0, tiled=True).reshape(
        ranks * slots, grid
    )
    wide = min(8, slots)
    partial, lists = call(
        matrix_kernel,
        (
            jax.ShapeDtypeStruct((ranks // 2, 2, columns, per_owner * piece, block), bf16),
            jax.ShapeDtypeStruct((ranks, block), f32),
        ),
        [SMEM, SMEM, rows_of(wide, width, grid), VMEM, VMEM, VMEM],
        [
            pltpu.VMEM((entries, block, block), f32),
            pltpu.VMEM((slots, grid), f32),
            pltpu.VMEM((ranks * stride, grid), f32),
        ],
        grid=(slots // wide,),
        limit=48,
        flops=slots * width * width * grid * 2,
        moved=slots * width * grid * 2,
    )(pairs, plan_rows, basis, rho, stored, grid_weights[:, 0])

    rows = per_owner * piece
    partial, spread = lax.optimization_barrier((partial, spread))
    received = lax.all_to_all(
        partial.reshape(ranks * columns, rows, block),
        ("batch", "blk"),
        split_axis=0,
        concat_axis=0,
        tiled=True,
    ).reshape(ranks * columns * rows, block)
    density = call(
        place_kernel,
        jax.ShapeDtypeStruct((slots, grid), f32),
        [VMEM, VMEM, SMEM],
        moved=ranks * slots * grid * 2,
    )(spread, load_plan, rank.reshape(1))

    targets = lists[:, :entries].astype(jnp.int32).reshape(ranks * entries, 1) * piece
    targets = (targets + jnp.arange(piece, dtype=jnp.int32)[None]).reshape(
        1, ranks * entries * piece
    )
    totals = call(
        add_kernel,
        jax.ShapeDtypeStruct((ranks, held * piece, block), bf16),
        [VMEM, VMEM],
        moved=ranks * columns * rows * block * 2,
    )(targets, received)
    gathered = lax.all_to_all(totals, "batch", split_axis=0, concat_axis=0, tiled=True)
    hamiltonian = call(
        merge_kernel,
        jax.ShapeDtypeStruct((held, block, block), f32),
        [VMEM],
        moved=held * block * block * 6,
    )(gathered.reshape(ranks // 2, 2, held * piece, block))
    return (hamiltonian, density[:, None, :])


def solution(mesh):
    return jax.shard_map(
        on_device,
        mesh=mesh,
        in_specs=(
            P("batch", "blk", None, None),
            P("batch", "blk", None, None),
            P("batch", "blk", None),
            P("batch", "blk", None, None),
            P("batch", "blk", None),
            P("batch", "blk", None),
            P("blk", None),
            P("blk", None, None),
            P("batch", "blk", None, None),
            P("batch", "blk", None),
        ),
        out_specs=(P("blk", None, None), P("batch", "blk", None)),
        check_vma=False,
    )
```

```python
import jax
import jax.numpy as jnp
from jax import lax
from jax.experimental import pallas as pl
from jax.experimental.pallas import tpu as pltpu
from jax.sharding import PartitionSpec as P

LIST = 3
BATCH = ("z", "x")
xc_scale = 0.98474502
soft_square = 0.01
zero_exchange = xc_scale * soft_square ** (1.0 / 6.0)
log2_e = 1.4426950408889634

bf16 = jnp.bfloat16
f32 = jnp.float32
VMEM = pl.BlockSpec(memory_space=pltpu.VMEM)
HBM = pl.BlockSpec(memory_space=pltpu.HBM)
SMEM = pl.BlockSpec(memory_space=pltpu.SMEM)


def rows_of(*block):
    return pl.BlockSpec(block, lambda n: (n,) + (0,) * (len(block) - 1))


def call(body, outs, ins, scratch=(), flops=0, moved=0, limit=24, grid=(), out_specs=None):
    return pl.pallas_call(
        body,
        out_shape=outs,
        grid=grid,
        in_specs=ins,
        out_specs=out_specs or jax.tree.map(lambda _: VMEM, outs),
        scratch_shapes=list(scratch),
        compiler_params=pltpu.CompilerParams(vmem_limit_bytes=limit * 2**20),
        cost_estimate=pl.CostEstimate(flops=flops, bytes_accessed=moved, transcendentals=0),
    )


def in_parts(value):
    high = value.astype(bf16).astype(f32)
    rest = value - high
    middle = rest.astype(bf16).astype(f32)
    return high, middle, rest - middle


LEFT = (0, 1, 2, 0, 1, 0)
RIGHT = (0, 0, 0, 1, 1, 2)
TERMS = 32


def basis_kernel(
    points_ref, centers_ref, exponents_ref, angular_ref, out_ref, done_ref, left_ref, right_ref
):
    slots = out_ref.shape[0]
    chunks, total, lanes = left_ref.shape
    total //= TERMS
    chunks //= 2
    halves = right_ref.shape[0]

    @pl.when(pl.program_id(0) == 0)
    def _():
        done_ref[...] = jnp.zeros_like(done_ref)
        none = jnp.zeros((total, lanes), f32)

        def put(ref, at, row, value):
            ref[at, pl.ds(row, total, TERMS), :] = value

        for j in range(chunks):
            scale = exponents_ref[pl.ds(j, total, chunks), :] * -log2_e
            center, slope = [], []
            for a in range(3):
                center.append(centers_ref[pl.ds(a * chunks + j, total, 3 * chunks), :])
                slope.append(angular_ref[pl.ds(a * chunks + j, total, 3 * chunks), :])
            square = center[0] * center[0] + center[1] * center[1] + center[2] * center[2]
            offset = slope[0] * center[0] + slope[1] * center[1] + slope[2] * center[2]
            logarithm = [scale] + [(-2.0 * scale) * c for c in center] + [scale * square]
            factor = [None] + slope + [1.0 - offset]
            for at, values in ((j, logarithm), (chunks + j, factor)):
                for n in range(5):
                    parts = (none, none, none) if values[n] is None else in_parts(values[n])
                    for i in range(6 if n < 4 else 3):
                        put(left_ref, at, 6 * n + i, parts[LEFT[i]])
                for row in range(27, TERMS):
                    put(left_ref, at, row, none)
        for j in range(halves):
            point = [points_ref[pl.ds(a * halves + j, total, 3 * halves), :] for a in range(3)]
            square = point[0] * point[0] + point[1] * point[1] + point[2] * point[2]
            for n, value in enumerate([square] + point):
                parts = in_parts(value)
                for i in range(6):
                    put(right_ref, j, 6 * n + i, parts[RIGHT[i]])
            for row in range(24, TERMS):
                put(right_ref, j, row, none + 1.0 if row < 27 else none)

    start = pl.program_id(0) * slots
    for s in range(slots):
        rows = pl.ds((start + s) * TERMS, TERMS)
        right = jnp.concatenate([right_ref[j, rows, :] for j in range(halves)], axis=1).astype(bf16)
        for j in range(chunks):
            found = [
                lax.dot_general(
                    left_ref[at, rows, :].astype(bf16),
                    right,
                    (((0,), (0,)), ((), ())),
                    preferred_element_type=f32,
                )
                for at in (j, chunks + j)
            ]
            value = jnp.exp2(found[0]) * found[1]
            out_ref[s, j * lanes : (j + 1) * lanes, :] = value.astype(bf16)


def pick_kernel(asked_ref, blocks_ref, out_ref):
    per_owner = asked_ref.shape[2]
    for e in range(out_ref.shape[0]):
        out_ref[e] = blocks_ref[asked_ref[e // per_owner, 0, e % per_owner]]


def spread_kernel(hartree_ref, listed_ref, done_ref, out_ref):
    del done_ref
    rows, grid = out_ref.shape
    below = jnp.broadcast_to(listed_ref[...], (rows - hartree_ref.shape[0], grid))
    out_ref[...] = jnp.concatenate([hartree_ref[...] - zero_exchange, below]).astype(bf16)


def density_kernel(pairs_ref, basis_ref, table_ref, rho_ref, copies_ref, sub_ref):
    slots = basis_ref.shape[0]
    block = table_ref.shape[1]
    unroll = sub_ref.shape[0]
    start = pl.program_id(0) * slots

    def group(turn, carry):
        for u in range(unroll):
            s = turn * unroll + u
            for k in range(LIST):
                for l in range(LIST):
                    sub_ref[u, k * block : (k + 1) * block, l * block : (l + 1) * block] = table_ref[
                        pairs_ref[(start + s) * LIST * LIST + k * LIST + l]
                    ]
        for u in range(unroll):
            s = turn * unroll + u
            basis = basis_ref[s]
            inner = jnp.dot(sub_ref[u], basis, preferred_element_type=f32)
            rho_ref[pl.ds(start + s, 1), :] = jnp.sum(inner * basis.astype(f32), axis=0, keepdims=True)
        return carry

    lax.fori_loop(0, slots // unroll, group, 0)

    @pl.when(start == rho_ref.shape[0] - slots)
    def _():
        sent = rho_ref[...].astype(bf16)
        for h in range(copies_ref.shape[0]):
            copies_ref[h] = sent


def matrix_kernel(
    pairs_ref, plan_ref, basis_ref, rho_ref, hartree_ref, weights_ref,
    out_ref, lists_ref, sums_ref, factor_ref, stored_ref,
):
    slots = basis_ref.shape[0]
    total = rho_ref.shape[0]
    entries, block, _ = sums_ref.shape
    stride = hartree_ref.shape[1]
    unroll = slots
    start = pl.program_id(0) * slots

    @pl.when(start == 0)
    def _():
        for r in range(lists_ref.shape[0]):
            lines = hartree_ref[r].astype(f32)
            stored_ref[r * stride : (r + 1) * stride, :] = lines
            lists_ref[r : r + 1, :] = lines[total : total + 1, :block]
        for s in range(total):
            at = plan_ref[s]
            factor_ref[s : s + 1, :] = stored_ref[
                pl.ds(lax.div(at, total) * stride + lax.rem(at, total), 1), :
            ]
        rho = rho_ref[...]
        root = jnp.exp2(jnp.log2(rho * rho + soft_square) * (1.0 / 6.0))
        factor_ref[...] = weights_ref[...] * (factor_ref[...] + (zero_exchange - xc_scale * root))

        def clear(e, carry):
            sums_ref[e] = jnp.zeros((block, block), f32)
            return carry

        lax.fori_loop(0, entries, clear, 0)

    def group(turn, carry):
        for u in range(unroll):
            s = turn * unroll + u
            basis = basis_ref[s]
            scaled = (basis.astype(f32) * factor_ref[pl.ds(start + s, 1), :]).astype(bf16)
            full = lax.dot_general(
                basis, scaled, (((1,), (1,)), ((), ())), preferred_element_type=f32
            )
            for k in range(LIST):
                for l in range(LIST):
                    e = pairs_ref[(start + s) * LIST * LIST + k * LIST + l]
                    sums_ref[e] += full[
                        k * block : (k + 1) * block, l * block : (l + 1) * block
                    ]
        return carry

    lax.fori_loop(0, slots // unroll, group, 0)

    @pl.when(start == total - slots)
    def _():
        low = lax.broadcasted_iota(jnp.int32, (1, 8, block), 1) < 4
        for c in range(out_ref.shape[2]):
            first = sums_ref[2 * c].reshape(block // 8, 8, block)
            second = sums_ref[2 * c + 1].reshape(block // 8, 8, block)
            out_ref[:, 0, c] = jnp.where(low, first, pltpu.roll(second, 4, 1)).astype(bf16)
            out_ref[:, 1, c] = jnp.where(low, pltpu.roll(first, 4, 1), second).astype(bf16)


def add_kernel(target_ref, received_ref, out_ref):
    rows = out_ref.shape[1]
    length = target_ref.shape[1]
    chosen = lax.broadcasted_iota(jnp.int32, (rows, length), 0) == target_ref[...]
    total = jnp.dot(
        chosen.astype(f32).astype(bf16), received_ref[...], preferred_element_type=f32
    ).astype(bf16)
    for h in range(out_ref.shape[0]):
        out_ref[h] = total


def place_kernel(spread_ref, plan_ref, rank_ref, density_ref):
    slots = density_ref.shape[0]
    length = plan_ref.shape[1]
    own = lax.broadcasted_iota(jnp.int32, (slots, length), 0) + rank_ref[0] * slots
    chosen = (own == plan_ref[...]).astype(f32).astype(bf16)
    density_ref[...] = jnp.dot(chosen, spread_ref[...], preferred_element_type=f32)


def merge_kernel(received_ref, out_ref):
    half, _, rows, block = received_ref.shape
    low = lax.broadcasted_iota(jnp.int32, (1, 8, block), 1) < 4
    for at in range(0, rows, 16):
        even = received_ref[:, 0, at : at + 16, :].astype(f32)
        odd = received_ref[:, 1, at : at + 16, :].astype(f32)
        for q in range(2):
            first = even[:, 8 * q : 8 * q + 8]
            second = odd[:, 8 * q : 8 * q + 8]
            place = at // 4 + 2 * q
            out_ref[place] = jnp.where(low, first, pltpu.roll(second, 4, 1)).reshape(8 * half, block)
            out_ref[place + 1] = jnp.where(low, pltpu.roll(first, 4, 1), second).reshape(
                8 * half, block
            )


def on_device(
    points,
    centers,
    exponents,
    angular,
    grid_weights,
    hartree,
    load_plan,
    density_blocks,
    pair_lists,
    batch_pairs,
):
    slots, _, _, grid = points.shape
    ranks = lax.axis_size(BATCH)
    columns = lax.axis_size("blk")
    per_owner = pair_lists.shape[3]
    held, block, _ = density_blocks.shape
    entries = columns * per_owner
    width = LIST * block
    piece = block // ranks
    rank = lax.axis_index(BATCH)
    plan_rows = lax.dynamic_slice_in_dim(load_plan[0], rank * slots, slots)

    wanted = pair_lists.reshape(columns, 1, per_owner)
    asked = lax.all_to_all(wanted, "blk", split_axis=0, concat_axis=0, tiled=True)
    sent = call(
        pick_kernel,
        jax.ShapeDtypeStruct((entries, block, block), bf16),
        [SMEM, VMEM],
        moved=entries * block * block * 4,
    )(asked, density_blocks)
    table = lax.all_to_all(
        sent.reshape(columns, per_owner * block, block), "blk", split_axis=0, concat_axis=0, tiled=True
    ).reshape(entries, block, block)

    group = min(4, slots)
    steps = (slots // group,)
    basis, done = call(
        basis_kernel,
        (jax.ShapeDtypeStruct((slots, width, grid), bf16), jax.ShapeDtypeStruct((8, block), f32)),
        [VMEM, VMEM, VMEM, VMEM],
        [
            pltpu.VMEM((2 * LIST, slots * TERMS, block), f32),
            pltpu.VMEM((grid // block, slots * TERMS, block), f32),
        ],
        grid=steps,
        out_specs=(rows_of(group, width, grid), VMEM),
        limit=48,
        flops=slots * width * grid * 400,
        moved=slots * width * grid * 2,
    )(
        points.reshape(-1, block),
        centers.reshape(-1, block),
        exponents.reshape(-1, block),
        angular.reshape(-1, block),
    )

    stride = slots + 8
    lines = call(
        spread_kernel,
        jax.ShapeDtypeStruct((stride, grid), bf16),
        [VMEM, VMEM, HBM],
    )(
        hartree[:, 0],
        jnp.pad(asked.reshape(1, entries).astype(f32), ((0, 0), (0, grid - entries))),
        done,
    )
    lines = lax.all_gather(lines, "x", axis=0, tiled=True)
    planes = lax.axis_size("z")
    stored = lax.all_to_all(
        jnp.broadcast_to(lines[None], (planes,) + lines.shape), "z", split_axis=0, concat_axis=0, tiled=True
    ).reshape(ranks, stride, grid)

    pairs = batch_pairs.reshape(slots * LIST * LIST)
    unroll = 2
    rho, copies = call(
        density_kernel,
        (
            jax.ShapeDtypeStruct((slots, grid), f32),
            jax.ShapeDtypeStruct((ranks, slots, grid), bf16),
        ),
        [SMEM, rows_of(group, width, grid), VMEM],
        [pltpu.VMEM((unroll, width, width), bf16)],
        grid=steps,
        limit=48,
        flops=slots * width * width * grid * 2,
        moved=slots * width * grid * 2,
    )(pairs, basis, table)
    spread = lax.all_to_all(copies, BATCH, split_axis=0, concat_axis=0, tiled=True).reshape(
        ranks * slots, grid
    )
    wide = min(8, slots)
    partial, lists = call(
        matrix_kernel,
        (
            jax.ShapeDtypeStruct((ranks // 2, 2, columns, per_owner * piece, block), bf16),
            jax.ShapeDtypeStruct((ranks, block), f32),
        ),
        [SMEM, SMEM, rows_of(wide, width, grid), VMEM, VMEM, VMEM],
        [
            pltpu.VMEM((entries, block, block), f32),
            pltpu.VMEM((slots, grid), f32),
            pltpu.VMEM((ranks * stride, grid), f32),
        ],
        grid=(slots // wide,),
        limit=48,
        flops=slots * width * width * grid * 2,
        moved=slots * width * grid * 2,
    )(pairs, plan_rows, basis, rho, stored, grid_weights[:, 0])

    rows = per_owner * piece
    partial, spread = lax.optimization_barrier((partial, spread))
    received = lax.all_to_all(
        partial.reshape(ranks * columns, rows, block),
        BATCH + ("blk",),
        split_axis=0,
        concat_axis=0,
        tiled=True,
    ).reshape(ranks * columns * rows, block)
    density = call(
        place_kernel,
        jax.ShapeDtypeStruct((slots, grid), f32),
        [VMEM, VMEM, SMEM],
        moved=ranks * slots * grid * 2,
    )(spread, load_plan, rank.reshape(1))

    targets = lists[:, :entries].astype(jnp.int32).reshape(ranks * entries, 1) * piece
    targets = (targets + jnp.arange(piece, dtype=jnp.int32)[None]).reshape(
        1, ranks * entries * piece
    )
    totals = call(
        add_kernel,
        jax.ShapeDtypeStruct((ranks, held * piece, block), bf16),
        [VMEM, VMEM],
        moved=ranks * columns * rows * block * 2,
    )(targets, received)
    gathered = lax.all_to_all(totals, BATCH, split_axis=0, concat_axis=0, tiled=True)
    hamiltonian = call(
        merge_kernel,
        jax.ShapeDtypeStruct((held, block, block), f32),
        [VMEM],
        moved=held * block * block * 6,
    )(gathered.reshape(ranks // 2, 2, held * piece, block))
    return (hamiltonian, density[:, None, :])


def solution(mesh):
    ranks, columns = mesh.devices.shape
    fine = jax.sharding.Mesh(mesh.devices.reshape(ranks // 4, 4, columns), BATCH + ("blk",))
    return jax.shard_map(
        on_device,
        mesh=fine,
        in_specs=(
            P(BATCH, "blk", None, None),
            P(BATCH, "blk", None, None),
            P(BATCH, "blk", None),
            P(BATCH, "blk", None, None),
            P(BATCH, "blk", None),
            P(BATCH, "blk", None),
            P("blk", None),
            P("blk", None, None),
            P(BATCH, "blk", None, None),
            P(BATCH, "blk", None),
        ),
        out_specs=(P("blk", None, None), P(BATCH, "blk", None)),
        check_vma=False,
    )
```
